32 devices in a mesh: section: 4 (over y, x), hid: 8 (over z, core).
Axes of the slice: x: 2, y: 2, z: 4, core: 2. Of those that a mesh axis runs over, the one named last changes fastest.
Arguments:
- layer_input: bfloat16 [4, 32, 4096], P('section', 'hid'), may hold values from -6 to 6
- hidden_grad: bfloat16 [4, 16, 7168], P('section', None, 'hid'), may hold values from -3 to 3
- gate_weight: bfloat16 [4, 4096, 7168], P('section', None, 'hid'), may hold values from -0.09375 to 0.09375
- up_weight: bfloat16 [4, 4096, 7168], P('section', None, 'hid'), may hold values from -0.09375 to 0.09375
- expert_ids: int32 [4, 32, 2], replicated, may hold values from 0 to 7, as said below
Outputs:
- grad_in: bfloat16 [4, 32, 4096], P('section', 'hid')
- grad_gate_weight: bfloat16 [4, 4096, 7168], P('section', None, 'hid')
The draws below stay inside these ranges and needn't reach their ends.
Inputs may be any that keep to these rules, and one draw needn't show every extreme that they name: `expert_ids`: each token names two different experts. In every aligned block of 4 tokens of one section, between 1 and 2 tokens name expert 0; in one section every block has exactly 2.
All inputs are finite; a program needn't handle non-finite values.
Results may differ from the reference program's by a relative error of at most 0.0049.
Values may be sent and summed in bfloat16 or wider, within the bound.
No kernel may reach another device: no remote copies, remote signals or barrier semaphores. Data moves between devices by JAX's collectives and lax.ppermute only.
A program may use at most 64 MiB of HBM per device.

```python
import jax
import jax.numpy as jnp
from jax import lax

D = 4096
FF = 7168
EXPERTS = 8
TOK_DEV = 4
K_DEV = 2
TOKENS = 32
CAP = 16
SECTIONS = 4
N_HID = 8


def draw_expert_ids(key, part):
    id_shape = (SECTIONS, TOKENS // TOK_DEV, TOK_DEV)
    count_shape = (SECTIONS, TOKENS // TOK_DEV, 1)
    key_count, key_full, key_order, key_side, key_first, key_pair = jax.random.split(key, 6)
    counts = jax.random.randint(key_count, count_shape, 1, TOK_DEV // 2 + 1)
    full_section = jax.random.randint(key_full, (), 0, SECTIONS)
    section_iota = lax.broadcasted_iota(jnp.int32, count_shape, 0)
    counts = jnp.where(section_iota == full_section, TOK_DEV // 2, counts)
    scores = jax.random.randint(key_order, id_shape, 0, 1 << 20) * TOK_DEV + lax.broadcasted_iota(jnp.int32, id_shape, 2)
    perm_order = jnp.argsort(scores, axis=2)
    token_rank = jnp.argsort(perm_order, axis=2)
    chosen = token_rank < counts
    first_id = jax.random.randint(key_first, id_shape, 1, EXPERTS)
    offset_step = jax.random.randint(key_pair, id_shape, 1, EXPERTS - 1)
    second = 1 + (first_id - 1 + offset_step) % (EXPERTS - 1)
    zero_side = jax.random.randint(key_side, id_shape, 0, 2)
    column_a = jnp.where(chosen & (zero_side == 0), 0, first_id)
    column_b = jnp.where(chosen, jnp.where(zero_side == 0, first_id, 0), second)
    both = jnp.stack([column_a, column_b], axis=-1)
    return both.reshape(SECTIONS, TOKENS, 2).astype(jnp.int32)


def levels(own_key, extent, cuts, low, largest):
    def one(dim, shards_of):
        draws = jax.random.uniform(jax.random.fold_in(jax.random.fold_in(own_key, 6), dim), (shards_of,), jnp.float32, low / len(cuts), largest / len(cuts))
        return jnp.repeat(jnp.exp(draws), extent[dim] // shards_of).reshape((-1,) + (1,) * (len(extent) - dim - 1))

    gain = one(*cuts[0])
    for cut in cuts[1:]:
        gain = gain * one(*cut)
    return gain


def centred(rng, extent, spread, limit, cuts=(), kind=jnp.bfloat16):
    entries = jax.random.normal(rng, extent, jnp.float32) * spread
    if len(cuts) > 0:
        entries = levels(rng, extent, cuts, -0.22, 0.18) * entries
    return jnp.clip(entries, min=-limit, max=limit).astype(kind)


def setup_inputs(seed: int = 0) -> dict:
    seeds = jax.random.split(jax.random.key(seed), 6)
    layer_input = centred(seeds[0], (SECTIONS, TOKENS, D), 1.0, 6.0, ((0, 4), (1, 8)))
    hidden_grad = centred(seeds[1], (SECTIONS, CAP, FF), 0.5, 3.0, ((0, 4), (2, 8)))
    gate_weight = centred(seeds[2], (SECTIONS, D, FF), D ** -0.5, 0.09375, ((0, 4), (2, 8)))
    up_weight = centred(seeds[3], (SECTIONS, D, FF), D ** -0.5, 0.09375, ((0, 4), (2, 8)))
    expert_ids = draw_expert_ids(jax.random.fold_in(seeds[5], 71), 0)
    return dict(layer_input=layer_input, hidden_grad=hidden_grad, gate_weight=gate_weight, up_weight=up_weight, expert_ids=expert_ids)


def slot_index(ids):
    chosen = jnp.any(ids == 0, axis=1).astype(jnp.int32)
    blocks = chosen.reshape(N_HID, TOK_DEV)
    slot_rank = (jnp.cumsum(blocks, axis=1) - blocks).reshape(TOKENS)
    owner_dev = jnp.arange(TOKENS, dtype=jnp.int32) // TOK_DEV
    return jnp.where(chosen == 1, owner_dev * K_DEV + slot_rank, CAP).astype(jnp.int32)


def one_section(inputs, hidden_grad, gate_weight, up_weight, ids):
    slot = slot_index(ids)
    slot_rows = jnp.zeros((CAP + 1, D), jnp.bfloat16).at[slot].set(inputs)[:CAP]
    gate_act = jnp.dot(slot_rows, gate_weight, preferred_element_type=jnp.float32)
    up_act = jnp.dot(slot_rows, up_weight, preferred_element_type=jnp.float32)
    sigmoid_gate = jax.nn.sigmoid(gate_act)
    hidden_float = hidden_grad.astype(jnp.float32)
    grad_gate_act = (hidden_float * up_act * sigmoid_gate * (1.0 + gate_act * (1.0 - sigmoid_gate))).astype(jnp.bfloat16)
    grad_up_act = (hidden_float * gate_act * sigmoid_gate).astype(jnp.bfloat16)
    slot_grad = (jnp.dot(grad_gate_act, gate_weight.T, preferred_element_type=jnp.float32)
                 + jnp.dot(grad_up_act, up_weight.T, preferred_element_type=jnp.float32)).astype(jnp.bfloat16)
    padded = jnp.concatenate([slot_grad, jnp.zeros((1, D), jnp.bfloat16)], axis=0)
    token_grad = padded[slot]
    weight_grad = jnp.dot(slot_rows.T, grad_gate_act, preferred_element_type=jnp.float32).astype(jnp.bfloat16)
    return token_grad, weight_grad


def reference(layer_input, hidden_grad, gate_weight, up_weight, expert_ids):
    token_list = []
    weight_list = []
    for section_num in range(SECTIONS):
        token_grad, weight_grad = one_section(layer_input[section_num], hidden_grad[section_num],
                                            gate_weight[section_num], up_weight[section_num], expert_ids[section_num])
        token_list.append(token_grad)
        weight_list.append(weight_grad)
    grad_in = jnp.roll(jnp.stack(token_list), -1, axis=0)
    return grad_in, jnp.stack(weight_list)
```

```python
import functools

import jax
import jax.numpy as jnp
from jax import lax
from jax.experimental import pallas as pl
from jax.experimental.pallas import tpu as pltpu
from jax.sharding import PartitionSpec as P

F32 = jnp.float32
BF16 = jnp.bfloat16
CORES = 2
CHIPS = 4
VMEM = pl.BlockSpec(memory_space=pltpu.VMEM)
ANY = pl.BlockSpec(memory_space=pl.ANY)


def moved(value, target):
    sections, hids = lax.axis_size("section"), lax.axis_size("hid")
    pairs = []
    for section in range(sections):
        for hid in range(hids):
            to_section, to_hid = target(section, hid)
            pairs.append((section * hids + hid, (to_section % sections) * hids + to_hid))
    return lax.ppermute(value, ("section", "hid"), pairs)


def to_other_core(value):
    return moved(value, lambda section, hid: (section, hid ^ 1))


def expert_kernel(table_ref, hidden_ref, *refs, n_blocks, chunk):
    block_refs = refs[:n_blocks]
    gate_ref, up_ref, slots_ref, grad_gate_ref, keep_ref, send_ref = refs[n_blocks:]
    rows = jnp.concatenate([ref[...].astype(F32) for ref in block_refs], axis=0).astype(BF16)
    slots = jnp.dot(table_ref[...], rows, preferred_element_type=F32).astype(BF16)
    slots_ref[...] = slots
    cap, width = slots.shape
    hidden = gate_ref.shape[1]
    gate_act = jnp.zeros((cap, hidden), F32)
    up_act = jnp.zeros((cap, hidden), F32)
    for at in range(0, width, chunk):
        part = slots[:, at : at + chunk]
        gate_act += jnp.dot(part, gate_ref[at : at + chunk, :], preferred_element_type=F32)
        up_act += jnp.dot(part, up_ref[at : at + chunk, :], preferred_element_type=F32)
    sigmoid_gate = jax.nn.sigmoid(gate_act)
    hidden_float = hidden_ref[...].astype(F32)
    grad_gate = (
        hidden_float * up_act * sigmoid_gate * (1.0 + gate_act * (1.0 - sigmoid_gate))
    ).astype(BF16)
    grad_up = (hidden_float * gate_act * sigmoid_gate).astype(BF16)
    grad_gate_ref[...] = grad_gate
    half = cap // 2
    contract_last = (((1,), (1,)), ((), ()))
    for at in range(0, width, chunk):
        total = lax.dot_general(
            grad_gate, gate_ref[at : at + chunk, :], contract_last, preferred_element_type=F32
        ) + lax.dot_general(
            grad_up, up_ref[at : at + chunk, :], contract_last, preferred_element_type=F32
        )
        keep_ref[:, at : at + chunk] = total[:half]
        send_ref[:, at : at + chunk] = total[half:].astype(send_ref.dtype)


def expert(table, hidden_grad, blocks, gate, up, send_dtype):
    cap, hidden = hidden_grad.shape
    width = gate.shape[0]
    return pl.pallas_call(
        functools.partial(expert_kernel, n_blocks=len(blocks), chunk=512),
        out_shape=(
            jax.ShapeDtypeStruct((cap, width), BF16),
            jax.ShapeDtypeStruct((cap, hidden), BF16),
            jax.ShapeDtypeStruct((cap // 2, width), F32),
            jax.ShapeDtypeStruct((cap // 2, width), send_dtype),
        ),
        in_specs=[VMEM] * (4 + len(blocks)),
        out_specs=(VMEM,) * 4,
        compiler_params=pltpu.CompilerParams(vmem_limit_bytes=44 << 20),
        cost_estimate=pl.CostEstimate(
            flops=8 * cap * width * hidden, bytes_accessed=4 * width * hidden, transcendentals=cap * hidden
        ),
        name="expert",
    )(table, hidden_grad, *blocks, gate, up)


def weight_kernel(slots_ref, grad_ref, out_ref):
    out_ref[...] = lax.dot_general(
        slots_ref[...], grad_ref[...], (((0,), (0,)), ((), ())), preferred_element_type=F32
    ).astype(out_ref.dtype)


def weight_gradient(slots, grad_gate):
    cap, width = slots.shape
    hidden = grad_gate.shape[1]
    chunk = 512
    return pl.pallas_call(
        weight_kernel,
        out_shape=jax.ShapeDtypeStruct((width, hidden), BF16),
        grid=(width // chunk,),
        in_specs=[
            pl.BlockSpec((cap, chunk), lambda i: (0, i)),
            pl.BlockSpec((cap, hidden), lambda i: (0, 0)),
        ],
        out_specs=pl.BlockSpec((chunk, hidden), lambda i: (i, 0)),
        compiler_params=pltpu.CompilerParams(vmem_limit_bytes=16 << 20),
        cost_estimate=pl.CostEstimate(
            flops=2 * cap * width * hidden, bytes_accessed=2 * width * hidden, transcendentals=0
        ),
        name="weight_gradient",
    )(slots, grad_gate)


def slot_numbers(ids, tok_dev, k_dev):
    chosen = jnp.any(ids == 0, axis=1)
    blocks = chosen.reshape(-1, tok_dev).astype(jnp.int32)
    ranks = [jnp.zeros_like(blocks[:, 0])]
    for at in range(tok_dev - 1):
        ranks.append(ranks[-1] + blocks[:, at])
    rank = jnp.stack(ranks, axis=1).reshape(-1)
    owner = lax.broadcasted_iota(jnp.int32, rank.shape, 0) // tok_dev
    return jnp.where(chosen, owner * k_dev + rank, -1)


def permuted_table(slot_of, slot_ids, token_ids):
    tokens = lax.broadcasted_iota(jnp.int32, (1, slot_of.shape[0]), 1)
    picked = jnp.sum(jnp.where(token_ids[:, None] == tokens, slot_of[None, :], 0), axis=1)
    return (slot_ids[:, None] == picked[None, :]).astype(BF16)


def own_rows(slot_of, hid_at, tok_dev, k_dev, grads):
    token = lax.broadcasted_iota(jnp.int32, (tok_dev, 1), 0) + hid_at * tok_dev
    tokens = lax.broadcasted_iota(jnp.int32, (1, slot_of.shape[0]), 1)
    slot = jnp.sum(jnp.where(token == tokens, slot_of[None, :], 0), axis=1, keepdims=True)
    rows = jnp.zeros((tok_dev, grads.shape[1]), grads.dtype)
    for rank in range(k_dev):
        rows = jnp.where(slot == hid_at * k_dev + rank, grads[rank : rank + 1], rows)
    return rows


def per_device(layer_input, hidden_grad, gate_weight, up_weight, expert_ids):
    tok_dev = layer_input.shape[1]
    k_dev = tok_dev // 2
    section_at = lax.axis_index("section")
    hid_at = lax.axis_index("hid")
    sections, hids = lax.axis_size("section"), lax.axis_size("hid")
    split = hids == CORES * CHIPS
    core_at, chip_at = hid_at % CORES, hid_at // CORES
    own = layer_input[0]

    place = lax.broadcasted_iota(jnp.int32, (hids * tok_dev,), 0)
    device, token = place // tok_dev, place % tok_dev
    if split:
        other = to_other_core(own)
        near = moved(own, lambda section, hid: (section, hid ^ 2))
        both = jnp.concatenate([own, other], axis=0)
        far = moved(both, lambda section, hid: (section, hid ^ (4 if hid % CORES else 6)))
        near_other = to_other_core(near)
        far_other = to_other_core(far)
        blocks = [own, other, near, near_other, far, far_other]
        turn = jnp.where(device < 4, device, jnp.where(device < 6, device ^ 2, device ^ 3) ^ (2 * core_at))
        device = hid_at ^ turn
    else:
        blocks = [lax.all_gather(own, "hid", axis=0, tiled=True)]
    token_ids = device * tok_dev + token

    place = lax.broadcasted_iota(jnp.int32, (hids * k_dev,), 0)
    device, rank = place // k_dev, place % k_dev
    if split:
        quarter = device // CORES
        step = jnp.where(quarter < 2, core_at, 1 - core_at) + 2 * (quarter % 2)
        device = (chip_at ^ step) * CORES + device % CORES
    slot_ids = device * k_dev + rank

    ids = lax.dynamic_index_in_dim(expert_ids, section_at, 0, keepdims=False)
    table = permuted_table(slot_numbers(ids, tok_dev, k_dev), slot_ids, token_ids)
    slots_iota = lax.broadcasted_iota(jnp.int32, (1, hids * k_dev), 1)
    order = (slot_ids[:, None] == slots_iota).astype(BF16)
    hidden_ordered = jnp.dot(order, hidden_grad[0], preferred_element_type=F32).astype(BF16)

    slots, grad_gate, keep, send = expert(
        table, hidden_ordered, blocks, gate_weight[0], up_weight[0], BF16 if split else F32
    )

    next_ids = lax.dynamic_index_in_dim(expert_ids, (section_at + 1) % sections, 0, keepdims=False)
    if split:
        rows = keep.shape[0] // 2
        keep = keep + to_other_core(send).astype(F32)
        across = moved(keep[rows:].astype(BF16), lambda section, hid: (section, hid ^ 4))
        part = (keep[:rows] + across.astype(F32)).astype(BF16)
        part = moved(part, lambda section, hid: (section - 1, hid ^ (2 * (hid % CORES))))
        total = part.astype(F32) + to_other_core(part).astype(F32)
        own_total = jnp.where(core_at == 0, total[: rows // 2], total[rows // 2 :])
    else:
        whole = jnp.concatenate([keep, send], axis=0)
        own_total = lax.psum_scatter(whole, "hid", scatter_dimension=0, tiled=True)
        own_total = moved(own_total, lambda section, hid: (section - 1, hid))
    grad_in = own_rows(slot_numbers(next_ids, tok_dev, k_dev), hid_at, tok_dev, k_dev, own_total).astype(BF16)
    weight_grad = weight_gradient(slots, grad_gate)
    return (grad_in[None], weight_grad[None])


def solution(mesh):
    return jax.shard_map(
        per_device,
        mesh=mesh,
        in_specs=(
            P("section", "hid", None),
            P("section", None, "hid"),
            P("section", None, "hid"),
            P("section", None, "hid"),
            P(),
        ),
        out_specs=(P("section", "hid", None), P("section", None, "hid")),
        check_vma=False,
    )
```

```python
import functools

import jax
import jax.numpy as jnp
from jax import lax
from jax.experimental import pallas as pl
from jax.experimental.pallas import tpu as pltpu
from jax.sharding import PartitionSpec as P

F32 = jnp.float32
BF16 = jnp.bfloat16
CORES = 2
CHIPS = 4
VMEM = pl.BlockSpec(memory_space=pltpu.VMEM)
HBM = pl.BlockSpec(memory_space=pltpu.HBM)
ANY = pl.BlockSpec(memory_space=pl.ANY)


def moved(value, target):
    sections, hids = lax.axis_size("section"), lax.axis_size("hid")
    pairs = []
    for section in range(sections):
        for hid in range(hids):
            to_section, to_hid = target(section, hid)
            pairs.append((section * hids + hid, (to_section % sections) * hids + to_hid))
    return lax.ppermute(value, ("section", "hid"), pairs)


def to_other_core(value):
    return moved(value, lambda section, hid: (section, hid ^ 1))


def lanes(shape, dimension=1):
    return lax.broadcasted_iota(jnp.int32, shape, dimension)


def slot_row(ids_ref, section, tok_dev, k_dev):
    ids = ids_ref[pl.ds(section, 1)][0]
    tokens = ids.shape[1]
    chosen = jnp.where((ids[0:1] == 0) | (ids[1:2] == 0), 1.0, 0.0)
    chosen = jnp.broadcast_to(chosen, (8, tokens))
    before, after = lanes((tokens, tokens), 0), lanes((tokens, tokens), 1)
    earlier = jnp.where((before // tok_dev == after // tok_dev) & (before < after), 1.0, 0.0)
    rank = jnp.dot(chosen.astype(BF16), earlier.astype(BF16), preferred_element_type=F32)
    owner = (lanes((8, tokens)) // tok_dev).astype(F32)
    return jnp.where(chosen > 0, owner * k_dev + rank, -1.0)


def slot_at(slot_of, token):
    tokens = slot_of.shape[1]
    place = jnp.where(lanes((tokens, token.shape[1]), 0) == token, 1.0, 0.0).astype(BF16)
    return jnp.dot(slot_of.astype(BF16), place, preferred_element_type=F32)[0:1]


def pack_kernel(ids_ref, own_ref, other_ref, after_ref, out_ref, *, tok_dev, k_dev):
    del after_ref
    hid_at = lax.axis_index("hid")
    slot_of = slot_row(ids_ref, lax.axis_index("section"), tok_dev, k_dev)
    column = lanes((1, 2 * tok_dev))
    slots = slot_at(slot_of, (hid_at ^ (column // tok_dev)) * tok_dev + column % tok_dev)
    row = lanes((2 * k_dev, 1), 0)
    wanted = (hid_at ^ (row // k_dev)) * k_dev + row % k_dev
    table = jnp.where(wanted.astype(F32) == slots, 1.0, 0.0).astype(BF16)
    rows = jnp.concatenate([own_ref[...].astype(F32), other_ref[...].astype(F32)], axis=0)
    out_ref[...] = jnp.dot(table, rows.astype(BF16), preferred_element_type=F32).astype(BF16)


def pack(ids, own, other, after, k_dev):
    tok_dev, width = own.shape
    return pl.pallas_call(
        functools.partial(pack_kernel, tok_dev=tok_dev, k_dev=k_dev),
        out_shape=jax.ShapeDtypeStruct((2 * k_dev, width), BF16),
        in_specs=[VMEM] * 3 + [ANY],
        out_specs=VMEM,
        compiler_params=pltpu.CompilerParams(vmem_limit_bytes=4 << 20),
        name="pack",
    )(ids, own, other, after)


def open_kernel(out_ref):
    out_ref[...] = jnp.zeros_like(out_ref)


def opening(weight_bytes):
    return pl.pallas_call(
        open_kernel,
        out_shape=jax.ShapeDtypeStruct((8, 128), F32),
        out_specs=VMEM,
        compiler_params=pltpu.CompilerParams(vmem_limit_bytes=1 << 20),
        cost_estimate=pl.CostEstimate(flops=1000 * weight_bytes, bytes_accessed=2 * weight_bytes, transcendentals=0),
        name="opening",
    )()


def prepare_kernel(ids_ref, hidden_ref, after_ref, table_ref, hidden_out_ref, pick_ref, *, tok_dev, k_dev, split):
    del after_ref
    section_at, hid_at = lax.axis_index("section"), lax.axis_index("hid")
    core_at, chip_at = hid_at % CORES, hid_at // CORES
    cap, columns = table_ref.shape

    row = lanes((cap, 1), 0)
    device, rank = row // k_dev, row % k_dev
    if split:
        quarter = device // CORES
        step = 2 * jnp.where(quarter < 2, core_at, 1 - core_at) + quarter % 2
        device = (chip_at ^ step) * CORES + device % CORES
    wanted = device * k_dev + rank

    slot_of = slot_row(ids_ref, section_at, tok_dev, k_dev)
    column = lanes((1, columns))
    group, place = column // tok_dev, column % tok_dev
    if split:
        slots = slot_at(slot_of, (hid_at ^ (group + 1)) * tok_dev + place)
        turn = jnp.where(group == 0, 0, jnp.where(group == 3, 6 - 2 * core_at, 5 + 2 * core_at))
        packed = (hid_at ^ turn ^ (place // k_dev)) * k_dev + place % k_dev
        slots = jnp.where((group == 1) | (group == 2), slots, packed.astype(F32))
    else:
        slots = slot_at(slot_of, column)
    table_ref[...] = jnp.where(wanted.astype(F32) == slots, 1.0, 0.0).astype(BF16)

    order = jnp.where(wanted == lanes((cap, cap)), 1.0, 0.0).astype(BF16)
    hidden_out_ref[...] = jnp.dot(order, hidden_ref[...], preferred_element_type=F32).astype(BF16)

    sections = ids_ref.shape[0]
    slot_of = slot_row(ids_ref, (section_at + 1) % sections, tok_dev, k_dev)[0:1]
    token = lanes((tok_dev, slot_of.shape[1]), 0) + hid_at * tok_dev
    mine = jnp.where(lanes(token.shape) == token, slot_of, 0.0)
    mine = jnp.sum(mine, axis=1, keepdims=True) - (hid_at * k_dev).astype(F32)
    pick_ref[...] = jnp.broadcast_to(mine, pick_ref.shape)


def prepare(ids, hidden_grad, after, columns, tok_dev, k_dev, split):
    cap, hidden = hidden_grad.shape
    return pl.pallas_call(
        functools.partial(prepare_kernel, tok_dev=tok_dev, k_dev=k_dev, split=split),
        out_shape=(
            jax.ShapeDtypeStruct((cap, columns), BF16),
            jax.ShapeDtypeStruct((cap, hidden), BF16),
            jax.ShapeDtypeStruct((tok_dev, 128), F32),
        ),
        in_specs=[VMEM, VMEM, ANY],
        out_specs=(VMEM,) * 3,
        compiler_params=pltpu.CompilerParams(vmem_limit_bytes=4 << 20),
        name="prepare",
    )(ids, hidden_grad, after)


CONTRACT_LAST = (((1,), (1,)), ((), ()))


def expert_kernel(
    table_ref, hidden_ref, gate_ref, up_ref, *refs, n_blocks, chunk
):
    block_refs = refs[:n_blocks]
    slots_ref, grad_gate_ref, keep_ref, send_ref = refs[n_blocks:]
    rows = jnp.concatenate([ref[...].astype(F32) for ref in block_refs], axis=0).astype(BF16)
    slots = jnp.dot(table_ref[...], rows, preferred_element_type=F32).astype(BF16)
    slots_ref[...] = slots
    cap, width = slots.shape
    half = cap // 2
    gate_act = jnp.zeros((cap, gate_ref.shape[1]), F32)
    up_act = jnp.zeros((cap, gate_ref.shape[1]), F32)
    for at in range(0, width, chunk):
        part = slots[:, at : at + chunk]
        gate_act += jnp.dot(part, gate_ref[at : at + chunk, :], preferred_element_type=F32)
        up_act += jnp.dot(part, up_ref[at : at + chunk, :], preferred_element_type=F32)
    sigmoid_gate = jax.nn.sigmoid(gate_act)
    hidden_float = hidden_ref[...].astype(F32)
    grad_gate = (
        hidden_float * up_act * sigmoid_gate * (1.0 + gate_act * (1.0 - sigmoid_gate))
    ).astype(BF16)
    grad_up = (hidden_float * gate_act * sigmoid_gate).astype(BF16)
    grad_gate_ref[...] = grad_gate
    for at in range(0, width, chunk):
        there = slice(at, at + chunk)
        total = lax.dot_general(grad_gate, gate_ref[there, :], CONTRACT_LAST, preferred_element_type=F32)
        total += lax.dot_general(grad_up, up_ref[there, :], CONTRACT_LAST, preferred_element_type=F32)
        keep_ref[:, there] = total[:half]
        send_ref[:, there] = total[half:].astype(send_ref.dtype)


def expert(table, hidden_grad, gate, up, blocks, send_dtype):
    cap, hidden = hidden_grad.shape
    width = gate.shape[0]
    return pl.pallas_call(
        functools.partial(expert_kernel, n_blocks=len(blocks), chunk=512),
        out_shape=(
            jax.ShapeDtypeStruct((cap, width), BF16),
            jax.ShapeDtypeStruct((cap, hidden), BF16),
            jax.ShapeDtypeStruct((cap // 2, width), F32),
            jax.ShapeDtypeStruct((cap // 2, width), send_dtype),
        ),
        in_specs=[VMEM] * (4 + len(blocks)),
        out_specs=(VMEM,) * 4,
        compiler_params=pltpu.CompilerParams(vmem_limit_bytes=24 << 20),
        cost_estimate=pl.CostEstimate(
            flops=8 * cap * width * hidden, bytes_accessed=4 * width * hidden, transcendentals=cap * hidden
        ),
        name="expert",
    )(table, hidden_grad, gate, up, *blocks)


def weight_kernel(slots_ref, grad_ref, *refs, low, high, chunk):
    out_hbm, out_ref, sems = refs[-3:]
    copies = []
    for number, at in enumerate(range(low, high, chunk)):
        there = slice(at - low, at - low + chunk)
        out_ref[there, :] = lax.dot_general(
            slots_ref[:, at : at + chunk], grad_ref[...], (((0,), (0,)), ((), ())), preferred_element_type=F32
        ).astype(out_ref.dtype)
        copies.append(pltpu.make_async_copy(out_ref.at[there, :], out_hbm.at[at : at + chunk, :], sems.at[number]))
        copies[-1].start()
    for copy in copies:
        copy.wait()


def weight_gradient(slots, grad_gate, low, high, out=None):
    cap, width = slots.shape
    hidden = grad_gate.shape[1]
    chunk = 512
    return pl.pallas_call(
        functools.partial(weight_kernel, low=low, high=high, chunk=chunk),
        out_shape=jax.ShapeDtypeStruct((width, hidden), BF16),
        in_specs=[VMEM, VMEM] + ([] if out is None else [HBM]),
        out_specs=HBM,
        scratch_shapes=[
            pltpu.VMEM((high - low, hidden), BF16),
            pltpu.SemaphoreType.DMA(((high - low) // chunk,)),
        ],
        input_output_aliases={} if out is None else {2: 0},
        compiler_params=pltpu.CompilerParams(vmem_limit_bytes=12 << 20),
        cost_estimate=pl.CostEstimate(
            flops=2 * cap * (high - low) * hidden, bytes_accessed=2 * (high - low) * hidden, transcendentals=0
        ),
        name="weight_gradient",
    )(slots, grad_gate, *([] if out is None else [out]))


def per_device(layer_input, hidden_grad, gate_weight, up_weight, expert_ids):
    tok_dev = layer_input.shape[1]
    k_dev = tok_dev // 2
    hids = lax.axis_size("hid")
    split = hids == CORES * CHIPS
    core_at = lax.axis_index("hid") % CORES
    own, gate, up = layer_input[0], gate_weight[0], up_weight[0]
    ids = jnp.swapaxes(expert_ids, 1, 2)

    if split:
        start = opening(4 * gate.size)
        own, start = lax.optimization_barrier((own, start))
        other = to_other_core(own)
        near = moved(own, lambda section, hid: (section, hid ^ 2))
        both = pack(ids, own, other, start, k_dev)
        far = moved(both, lambda section, hid: (section, hid ^ (4 if hid % CORES else 6)))
        blocks = [both, near, to_other_core(near), far, to_other_core(far)]
        after = both
    else:
        blocks = [lax.all_gather(own, "hid", axis=0, tiled=True)]
        after = own
    columns = sum(block.shape[0] for block in blocks)
    table, hidden_ordered, pick = prepare(ids, hidden_grad[0], after, columns, tok_dev, k_dev, split)
    slots, grad_gate, keep, send = expert(
        table, hidden_ordered, gate, up, blocks, BF16 if split else F32
    )
    width = gate.shape[0]

    if split:
        rows = keep.shape[0] // 2
        keep = keep + to_other_core(send).astype(F32)
        keep, slots, grad_gate = lax.optimization_barrier((keep, slots, grad_gate))
        across = moved(keep[rows:].astype(BF16), lambda section, hid: (section, hid ^ 2))
        weight_grad = weight_gradient(slots, grad_gate, 0, width)
        across, weight_grad = lax.optimization_barrier((across, weight_grad))
        part = (keep[:rows] + across.astype(F32)).astype(BF16)
        part, slots = lax.optimization_barrier((part, slots))
        part = moved(part, lambda section, hid: (section - 1, hid ^ (4 * (hid % CORES))))
        part, weight_grad = lax.optimization_barrier((part, weight_grad))
        total = part.astype(F32) + to_other_core(part).astype(F32)
        own_total = jnp.where(core_at == 0, total[:k_dev], total[k_dev:])
    else:
        weight_grad = weight_gradient(slots, grad_gate, 0, width)
        whole = jnp.concatenate([keep, send], axis=0)
        own_total = lax.psum_scatter(whole, "hid", scatter_dimension=0, tiled=True)
        own_total = moved(own_total, lambda section, hid: (section - 1, hid))
    grad_in = jnp.zeros((tok_dev, own.shape[1]), F32)
    for rank in range(k_dev):
        grad_in = jnp.where(pick[:, :1] == rank, own_total[rank : rank + 1], grad_in)
    return (grad_in.astype(BF16)[None], weight_grad[None])


def solution(mesh):
    return jax.shard_map(
        per_device,
        mesh=mesh,
        in_specs=(
            P("section", "hid", None),
            P("section", None, "hid"),
            P("section", None, "hid"),
            P("section", None, "hid"),
            P(),
        ),
        out_specs=(P("section", "hid", None), P("section", None, "hid")),
        check_vma=False,
    )
```

```python
import functools

import jax
import jax.numpy as jnp
from jax import lax
from jax.experimental import pallas as pl
from jax.experimental.pallas import tpu as pltpu
from jax.sharding import PartitionSpec as P

F32 = jnp.float32
BF16 = jnp.bfloat16
CORES = 2
CHIPS = 4
VMEM = pl.BlockSpec(memory_space=pltpu.VMEM)
HBM = pl.BlockSpec(memory_space=pltpu.HBM)
ANY = pl.BlockSpec(memory_space=pl.ANY)


def moved(value, target):
    sections, hids = lax.axis_size("section"), lax.axis_size("hid")
    pairs = []
    for section in range(sections):
        for hid in range(hids):
            to_section, to_hid = target(section, hid)
            pairs.append((section * hids + hid, (to_section % sections) * hids + to_hid))
    return lax.ppermute(value, ("section", "hid"), pairs)


def to_other_core(value):
    return moved(value, lambda section, hid: (section, hid ^ 1))


def lanes(shape, dimension=1):
    return lax.broadcasted_iota(jnp.int32, shape, dimension)


def slot_row(ids_ref, section, tok_dev, k_dev):
    ids = ids_ref[pl.ds(section, 1)][0]
    tokens = ids.shape[1]
    chosen = jnp.where((ids[0:1] == 0) | (ids[1:2] == 0), 1.0, 0.0)
    chosen = jnp.broadcast_to(chosen, (8, tokens))
    before, after = lanes((tokens, tokens), 0), lanes((tokens, tokens), 1)
    earlier = jnp.where((before // tok_dev == after // tok_dev) & (before < after), 1.0, 0.0)
    rank = jnp.dot(chosen.astype(BF16), earlier.astype(BF16), preferred_element_type=F32)
    owner = (lanes((8, tokens)) // tok_dev).astype(F32)
    return jnp.where(chosen > 0, owner * k_dev + rank, -1.0)


def slot_at(slot_of, token):
    tokens = slot_of.shape[1]
    place = jnp.where(lanes((tokens, token.shape[1]), 0) == token, 1.0, 0.0).astype(BF16)
    return jnp.dot(slot_of.astype(BF16), place, preferred_element_type=F32)[0:1]


def pack_kernel(ids_ref, own_ref, other_ref, after_ref, out_ref, *, tok_dev, k_dev):
    del after_ref
    hid_at = lax.axis_index("hid")
    slot_of = slot_row(ids_ref, lax.axis_index("section"), tok_dev, k_dev)
    column = lanes((1, 2 * tok_dev))
    slots = slot_at(slot_of, (hid_at ^ (column // tok_dev)) * tok_dev + column % tok_dev)
    row = lanes((2 * k_dev, 1), 0)
    wanted = (hid_at ^ (row // k_dev)) * k_dev + row % k_dev
    table = jnp.where(wanted.astype(F32) == slots, 1.0, 0.0).astype(BF16)
    rows = jnp.concatenate([own_ref[...].astype(F32), other_ref[...].astype(F32)], axis=0)
    out_ref[...] = jnp.dot(table, rows.astype(BF16), preferred_element_type=F32).astype(BF16)


def pack(ids, own, other, after, k_dev):
    tok_dev, width = own.shape
    return pl.pallas_call(
        functools.partial(pack_kernel, tok_dev=tok_dev, k_dev=k_dev),
        out_shape=jax.ShapeDtypeStruct((2 * k_dev, width), BF16),
        in_specs=[VMEM] * 3 + [ANY],
        out_specs=VMEM,
        compiler_params=pltpu.CompilerParams(vmem_limit_bytes=4 << 20),
        name="pack",
    )(ids, own, other, after)


def open_kernel(out_ref):
    out_ref[...] = jnp.zeros_like(out_ref)


def opening(weight_bytes):
    return pl.pallas_call(
        open_kernel,
        out_shape=jax.ShapeDtypeStruct((8, 128), F32),
        out_specs=VMEM,
        compiler_params=pltpu.CompilerParams(vmem_limit_bytes=1 << 20),
        cost_estimate=pl.CostEstimate(flops=1000 * weight_bytes, bytes_accessed=2 * weight_bytes, transcendentals=0),
        name="opening",
    )()


def prepare_kernel(
    ids_ref, hidden_ref, gate_ref, up_ref, after_ref, table_ref, hidden_out_ref, pick_ref, up_turned_ref,
    *, tok_dev, k_dev, split, chunk,
):
    del gate_ref, after_ref
    for at in range(0, up_ref.shape[0], chunk):
        up_turned_ref[:, at : at + chunk] = up_ref[at : at + chunk, :].T
    section_at, hid_at = lax.axis_index("section"), lax.axis_index("hid")
    core_at, chip_at = hid_at % CORES, hid_at // CORES
    cap, columns = table_ref.shape

    row = lanes((cap, 1), 0)
    device, rank = row // k_dev, row % k_dev
    if split:
        quarter = device // CORES
        step = 2 * jnp.where(quarter < 2, core_at, 1 - core_at) + quarter % 2
        device = (chip_at ^ step) * CORES + device % CORES
    wanted = device * k_dev + rank

    column = lanes((1, columns))
    if split:
        group, place = column // tok_dev, column % tok_dev
        turn = jnp.where(group < 2, 2 * group, jnp.where(group == 2, 6 - 2 * core_at, 5 + 2 * core_at))
        slots = (hid_at ^ turn ^ (place // k_dev)) * k_dev + place % k_dev
    else:
        slots = slot_at(slot_row(ids_ref, section_at, tok_dev, k_dev), column).astype(jnp.int32)
    table_ref[...] = jnp.where(wanted == slots, 1.0, 0.0).astype(BF16)

    order = jnp.where(wanted == lanes((cap, cap)), 1.0, 0.0).astype(BF16)
    hidden_out_ref[...] = jnp.dot(order, hidden_ref[...], preferred_element_type=F32).astype(BF16)

    sections = ids_ref.shape[0]
    slot_of = slot_row(ids_ref, (section_at + 1) % sections, tok_dev, k_dev)[0:1]
    token = lanes((tok_dev, slot_of.shape[1]), 0) + hid_at * tok_dev
    mine = jnp.where(lanes(token.shape) == token, slot_of, 0.0)
    mine = jnp.sum(mine, axis=1, keepdims=True) - (hid_at * k_dev).astype(F32)
    pick_ref[...] = jnp.broadcast_to(mine, pick_ref.shape)


def prepare(ids, hidden_grad, gate, up, after, columns, tok_dev, k_dev, split):
    cap, hidden = hidden_grad.shape
    return pl.pallas_call(
        functools.partial(prepare_kernel, tok_dev=tok_dev, k_dev=k_dev, split=split, chunk=512),
        out_shape=(
            jax.ShapeDtypeStruct((cap, columns), BF16),
            jax.ShapeDtypeStruct((cap, hidden), BF16),
            jax.ShapeDtypeStruct((tok_dev, 128), F32),
            jax.ShapeDtypeStruct((hidden, gate.shape[0]), BF16),
        ),
        in_specs=[VMEM] * 4 + [ANY],
        out_specs=(VMEM,) * 4,
        compiler_params=pltpu.CompilerParams(vmem_limit_bytes=4 << 20),
        cost_estimate=pl.CostEstimate(flops=0, bytes_accessed=4 * gate.size, transcendentals=0),
        name="prepare",
    )(ids, hidden_grad, gate, up, after)


def expert_kernel(
    table_ref, hidden_ref, gate_ref, up_ref, up_turned_ref, *refs, n_blocks, chunk
):
    block_refs = refs[:n_blocks]
    slots_ref, grad_gate_ref, keep_ref, send_ref, gate_turned_ref = refs[n_blocks:]
    rows = jnp.concatenate([ref[...].astype(F32) for ref in block_refs], axis=0).astype(BF16)
    slots = jnp.dot(table_ref[...], rows, preferred_element_type=F32).astype(BF16)
    slots_ref[...] = slots
    cap, width = slots.shape
    half = cap // 2
    gate_act = jnp.zeros((cap, gate_ref.shape[1]), F32)
    up_act = jnp.zeros((cap, gate_ref.shape[1]), F32)
    for at in range(0, width, chunk):
        part = slots[:, at : at + chunk]
        gate_act += jnp.dot(part, gate_ref[at : at + chunk, :], preferred_element_type=F32)
        up_act += jnp.dot(part, up_ref[at : at + chunk, :], preferred_element_type=F32)
        gate_turned_ref[:, at : at + chunk] = gate_ref[at : at + chunk, :].T
    sigmoid_gate = jax.nn.sigmoid(gate_act)
    hidden_float = hidden_ref[...].astype(F32)
    grad_gate = (
        hidden_float * up_act * sigmoid_gate * (1.0 + gate_act * (1.0 - sigmoid_gate))
    ).astype(BF16)
    grad_up = (hidden_float * gate_act * sigmoid_gate).astype(BF16)
    grad_gate_ref[...] = grad_gate
    for at in range(0, width, chunk):
        there = slice(at, at + chunk)
        total = jnp.dot(grad_gate, gate_turned_ref[:, there], preferred_element_type=F32)
        total += jnp.dot(grad_up, up_turned_ref[:, there], preferred_element_type=F32)
        keep_ref[:, there] = total[:half]
        send_ref[:, there] = total[half:].astype(send_ref.dtype)


def expert(table, hidden_grad, gate, up, up_turned, blocks, send_dtype):
    cap, hidden = hidden_grad.shape
    width = gate.shape[0]
    return pl.pallas_call(
        functools.partial(expert_kernel, n_blocks=len(blocks), chunk=512),
        out_shape=(
            jax.ShapeDtypeStruct((cap, width), BF16),
            jax.ShapeDtypeStruct((cap, hidden), BF16),
            jax.ShapeDtypeStruct((cap // 2, width), F32),
            jax.ShapeDtypeStruct((cap // 2, width), send_dtype),
        ),
        in_specs=[VMEM] * (5 + len(blocks)),
        out_specs=(VMEM,) * 4,
        scratch_shapes=[pltpu.VMEM((hidden, width), BF16)],
        compiler_params=pltpu.CompilerParams(vmem_limit_bytes=16 << 20),
        cost_estimate=pl.CostEstimate(
            flops=8 * cap * width * hidden, bytes_accessed=4 * width * hidden, transcendentals=cap * hidden
        ),
        name="expert",
    )(table, hidden_grad, gate, up, up_turned, *blocks)


def weight_kernel(slots_ref, grad_ref, *refs, low, high, chunk):
    out_hbm, out_ref, sems = refs[-3:]
    copies = []
    for number, at in enumerate(range(low, high, chunk)):
        there = slice(at - low, at - low + chunk)
        out_ref[there, :] = lax.dot_general(
            slots_ref[:, at : at + chunk], grad_ref[...], (((0,), (0,)), ((), ())), preferred_element_type=F32
        ).astype(out_ref.dtype)
        copies.append(pltpu.make_async_copy(out_ref.at[there, :], out_hbm.at[at : at + chunk, :], sems.at[number]))
        copies[-1].start()
    for copy in copies:
        copy.wait()


def weight_gradient(slots, grad_gate, low, high, out=None):
    cap, width = slots.shape
    hidden = grad_gate.shape[1]
    chunk = 256
    return pl.pallas_call(
        functools.partial(weight_kernel, low=low, high=high, chunk=chunk),
        out_shape=jax.ShapeDtypeStruct((width, hidden), BF16),
        in_specs=[VMEM, VMEM] + ([] if out is None else [HBM]),
        out_specs=HBM,
        scratch_shapes=[
            pltpu.VMEM((high - low, hidden), BF16),
            pltpu.SemaphoreType.DMA(((high - low) // chunk,)),
        ],
        input_output_aliases={} if out is None else {2: 0},
        compiler_params=pltpu.CompilerParams(vmem_limit_bytes=12 << 20),
        cost_estimate=pl.CostEstimate(
            flops=2 * cap * (high - low) * hidden, bytes_accessed=2 * (high - low) * hidden, transcendentals=0
        ),
        name="weight_gradient",
    )(slots, grad_gate, *([] if out is None else [out]))


def per_device(layer_input, hidden_grad, gate_weight, up_weight, expert_ids):
    tok_dev = layer_input.shape[1]
    k_dev = tok_dev // 2
    hids = lax.axis_size("hid")
    split = hids == CORES * CHIPS
    core_at = lax.axis_index("hid") % CORES
    own, gate, up = layer_input[0], gate_weight[0], up_weight[0]
    ids = jnp.swapaxes(expert_ids, 1, 2)

    if split:
        start = opening(4 * gate.size)
        other = to_other_core(own)
        both = pack(ids, own, other, start, k_dev)
        far = moved(both, lambda section, hid: (section, hid ^ (4 if hid % CORES else 6)))
        near = moved(both, lambda section, hid: (section, hid ^ 2))
        after = both
        columns = 4 * tok_dev
    else:
        after = own
        columns = hids * tok_dev
    table, hidden_ordered, pick, up_turned = prepare(
        ids, hidden_grad[0], gate, up, after, columns, tok_dev, k_dev, split
    )
    if split:
        far, up_turned = lax.optimization_barrier((far, up_turned))
        blocks = [both, near, far, to_other_core(far)]
    else:
        blocks = [lax.all_gather(own, "hid", axis=0, tiled=True)]
    slots, grad_gate, keep, send = expert(
        table, hidden_ordered, gate, up, up_turned, blocks, BF16 if split else F32
    )
    width = gate.shape[0]

    if split:
        rows, width = keep.shape[0] // 2, gate.shape[0]
        partner = to_other_core(send)
        keep = keep + partner.astype(F32)
        keep, slots, grad_gate = lax.optimization_barrier((keep, slots, grad_gate))
        across = moved(keep[rows:].astype(BF16), lambda section, hid: (section, hid ^ 2))
        weight_grad = weight_gradient(slots, grad_gate, 0 * width // 16, 9 * width // 16)
        across, weight_grad = lax.optimization_barrier((across, weight_grad))
        part = (keep[:rows] + across.astype(F32)).astype(BF16)
        part, slots = lax.optimization_barrier((part, slots))
        part = moved(part, lambda section, hid: (section - 1, hid ^ (4 * (hid % CORES))))
        weight_grad = weight_gradient(slots, grad_gate, 9 * width // 16, 16 * width // 16, weight_grad)
        part, weight_grad = lax.optimization_barrier((part, weight_grad))
        other = to_other_core(part)
        total = part.astype(F32) + other.astype(F32)
        own_total = jnp.where(core_at == 0, total[:k_dev], total[k_dev:])
    else:
        weight_grad = weight_gradient(slots, grad_gate, 0, width)
        whole = jnp.concatenate([keep, send], axis=0)
        own_total = lax.psum_scatter(whole, "hid", scatter_dimension=0, tiled=True)
        own_total = moved(own_total, lambda section, hid: (section - 1, hid))
    grad_in = jnp.zeros((tok_dev, own.shape[1]), F32)
    for rank in range(k_dev):
        grad_in = jnp.where(pick[:, :1] == rank, own_total[rank : rank + 1], grad_in)
    return (grad_in.astype(BF16)[None], weight_grad[None])


def solution(mesh):
    return jax.shard_map(
        per_device,
        mesh=mesh,
        in_specs=(
            P("section", "hid", None),
            P("section", None, "hid"),
            P("section", None, "hid"),
            P("section", None, "hid"),
            P(),
        ),
        out_specs=(P("section", "hid", None), P("section", None, "hid")),
        check_vma=False,
    )
```

```python
import functools

import jax
import jax.numpy as jnp
from jax import lax
from jax.experimental import pallas as pl
from jax.experimental.pallas import tpu as pltpu
from jax.sharding import PartitionSpec as P

F32 = jnp.float32
BF16 = jnp.bfloat16
CORES = 2
CHIPS = 4
VMEM = pl.BlockSpec(memory_space=pltpu.VMEM)
HBM = pl.BlockSpec(memory_space=pltpu.HBM)
ANY = pl.BlockSpec(memory_space=pl.ANY)


def moved(value, target):
    sections, hids = lax.axis_size("section"), lax.axis_size("hid")
    pairs = []
    for section in range(sections):
        for hid in range(hids):
            to_section, to_hid = target(section, hid)
            pairs.append((section * hids + hid, (to_section % sections) * hids + to_hid))
    return lax.ppermute(value, ("section", "hid"), pairs)


def to_other_core(value):
    return moved(value, lambda section, hid: (section, hid ^ 1))


def lanes(shape, dimension=1):
    return lax.broadcasted_iota(jnp.int32, shape, dimension)


def slot_row(ids_ref, section, tok_dev, k_dev):
    ids = ids_ref[pl.ds(section, 1)][0]
    tokens = ids.shape[1]
    chosen = jnp.where((ids[0:1] == 0) | (ids[1:2] == 0), 1.0, 0.0)
    chosen = jnp.broadcast_to(chosen, (8, tokens))
    before, after = lanes((tokens, tokens), 0), lanes((tokens, tokens), 1)
    earlier = jnp.where((before // tok_dev == after // tok_dev) & (before < after), 1.0, 0.0)
    rank = jnp.dot(chosen.astype(BF16), earlier.astype(BF16), preferred_element_type=F32)
    owner = (lanes((8, tokens)) // tok_dev).astype(F32)
    return jnp.where(chosen > 0, owner * k_dev + rank, -1.0)


def slot_at(slot_of, token):
    tokens = slot_of.shape[1]
    place = jnp.where(lanes((tokens, token.shape[1]), 0) == token, 1.0, 0.0).astype(BF16)
    return jnp.dot(slot_of.astype(BF16), place, preferred_element_type=F32)[0:1]


def pack_kernel(ids_ref, own_ref, other_ref, after_ref, out_ref, *, tok_dev, k_dev):
    del after_ref
    hid_at = lax.axis_index("hid")
    slot_of = slot_row(ids_ref, lax.axis_index("section"), tok_dev, k_dev)
    column = lanes((1, 2 * tok_dev))
    slots = slot_at(slot_of, (hid_at ^ (column // tok_dev)) * tok_dev + column % tok_dev)
    row = lanes((2 * k_dev, 1), 0)
    wanted = (hid_at ^ (row // k_dev)) * k_dev + row % k_dev
    table = jnp.where(wanted.astype(F32) == slots, 1.0, 0.0).astype(BF16)
    rows = jnp.concatenate([own_ref[...].astype(F32), other_ref[...].astype(F32)], axis=0)
    out_ref[...] = jnp.dot(table, rows.astype(BF16), preferred_element_type=F32).astype(BF16)


def pack(ids, own, other, after, k_dev):
    tok_dev, width = own.shape
    return pl.pallas_call(
        functools.partial(pack_kernel, tok_dev=tok_dev, k_dev=k_dev),
        out_shape=jax.ShapeDtypeStruct((2 * k_dev, width), BF16),
        in_specs=[VMEM] * 3 + [ANY],
        out_specs=VMEM,
        compiler_params=pltpu.CompilerParams(vmem_limit_bytes=4 << 20),
        name="pack",
    )(ids, own, other, after)


def open_kernel(out_ref):
    out_ref[...] = jnp.zeros_like(out_ref)


def opening(weight_bytes):
    return pl.pallas_call(
        open_kernel,
        out_shape=jax.ShapeDtypeStruct((8, 128), F32),
        out_specs=VMEM,
        compiler_params=pltpu.CompilerParams(vmem_limit_bytes=1 << 20),
        cost_estimate=pl.CostEstimate(flops=1000 * weight_bytes, bytes_accessed=2 * weight_bytes, transcendentals=0),
        name="opening",
    )()


def prepare_kernel(
    ids_ref, hidden_ref, gate_ref, up_ref, after_ref, table_ref, hidden_out_ref, pick_ref, up_turned_ref,
    *, tok_dev, k_dev, split, chunk,
):
    del gate_ref, after_ref
    for at in range(0, up_turned_ref.shape[1], chunk):
        up_turned_ref[:, at : at + chunk] = up_ref[at : at + chunk, :].T
    section_at, hid_at = lax.axis_index("section"), lax.axis_index("hid")
    core_at, chip_at = hid_at % CORES, hid_at // CORES
    cap, columns = table_ref.shape

    row = lanes((cap, 1), 0)
    device, rank = row // k_dev, row % k_dev
    if split:
        quarter = device // CORES
        step = 2 * jnp.where(quarter < 2, core_at, 1 - core_at) + quarter % 2
        device = (chip_at ^ step) * CORES + device % CORES
    wanted = device * k_dev + rank

    column = lanes((1, columns))
    if split:
        group, place = column // tok_dev, column % tok_dev
        turn = jnp.where(group < 2, 4 * group, jnp.where(group == 2, 2 + 4 * core_at, 7 - 4 * core_at))
        slots = (hid_at ^ turn ^ (place // k_dev)) * k_dev + place % k_dev
    else:
        slots = slot_at(slot_row(ids_ref, section_at, tok_dev, k_dev), column).astype(jnp.int32)
    table_ref[...] = jnp.where(wanted == slots, 1.0, 0.0).astype(BF16)

    order = jnp.where(wanted == lanes((cap, cap)), 1.0, 0.0).astype(BF16)
    hidden_out_ref[...] = jnp.dot(order, hidden_ref[...], preferred_element_type=F32).astype(BF16)

    sections = ids_ref.shape[0]
    slot_of = slot_row(ids_ref, (section_at + 1) % sections, tok_dev, k_dev)[0:1]
    token = lanes((tok_dev, slot_of.shape[1]), 0) + hid_at * tok_dev
    mine = jnp.where(lanes(token.shape) == token, slot_of, 0.0)
    mine = jnp.sum(mine, axis=1, keepdims=True) - (hid_at * k_dev).astype(F32)
    pick_ref[...] = jnp.broadcast_to(mine, pick_ref.shape)


def prepare(ids, hidden_grad, gate, up, after, columns, tok_dev, k_dev, split):
    cap, hidden = hidden_grad.shape
    return pl.pallas_call(
        functools.partial(prepare_kernel, tok_dev=tok_dev, k_dev=k_dev, split=split, chunk=512),
        out_shape=(
            jax.ShapeDtypeStruct((cap, columns), BF16),
            jax.ShapeDtypeStruct((cap, hidden), BF16),
            jax.ShapeDtypeStruct((tok_dev, 128), F32),
            jax.ShapeDtypeStruct((hidden, gate.shape[0] // 2), BF16),
        ),
        in_specs=[VMEM] * 4 + [ANY],
        out_specs=(VMEM,) * 4,
        compiler_params=pltpu.CompilerParams(vmem_limit_bytes=4 << 20),
        cost_estimate=pl.CostEstimate(flops=0, bytes_accessed=4 * gate.size, transcendentals=0),
        name="prepare",
    )(ids, hidden_grad, gate, up, after)


def turn_kernel(weight_ref, after_ref, out_ref, *, low, chunk):
    del after_ref
    for at in range(0, out_ref.shape[1], chunk):
        out_ref[:, at : at + chunk] = weight_ref[low + at : low + at + chunk, :].T


def turned(weight, after, low):
    width, hidden = weight.shape
    return pl.pallas_call(
        functools.partial(turn_kernel, low=low, chunk=512),
        out_shape=jax.ShapeDtypeStruct((hidden, width - low), BF16),
        in_specs=[VMEM, ANY],
        out_specs=VMEM,
        compiler_params=pltpu.CompilerParams(vmem_limit_bytes=4 << 20),
        cost_estimate=pl.CostEstimate(flops=0, bytes_accessed=4 * hidden * (width - low), transcendentals=0),
        name="turn",
    )(weight, after)


def expert_kernel(
    table_ref, hidden_ref, gate_ref, up_ref, low_turned_ref, high_turned_ref, *refs, n_blocks, chunk
):
    block_refs = refs[:n_blocks]
    slots_ref, grad_gate_ref, keep_ref, send_ref, gate_turned_ref = refs[n_blocks:]
    rows = jnp.concatenate([ref[...].astype(F32) for ref in block_refs], axis=0).astype(BF16)
    slots = jnp.dot(table_ref[...], rows, preferred_element_type=F32).astype(BF16)
    slots_ref[...] = slots
    cap, width = slots.shape
    half = cap // 2
    gate_act = jnp.zeros((cap, gate_ref.shape[1]), F32)
    up_act = jnp.zeros((cap, gate_ref.shape[1]), F32)
    for at in range(0, width, chunk):
        part = slots[:, at : at + chunk]
        gate_act += jnp.dot(part, gate_ref[at : at + chunk, :], preferred_element_type=F32)
        up_act += jnp.dot(part, up_ref[at : at + chunk, :], preferred_element_type=F32)
        gate_turned_ref[:, at : at + chunk] = gate_ref[at : at + chunk, :].T
    sigmoid_gate = jax.nn.sigmoid(gate_act)
    hidden_float = hidden_ref[...].astype(F32)
    grad_gate = (
        hidden_float * up_act * sigmoid_gate * (1.0 + gate_act * (1.0 - sigmoid_gate))
    ).astype(BF16)
    grad_up = (hidden_float * gate_act * sigmoid_gate).astype(BF16)
    grad_gate_ref[...] = grad_gate
    for at in range(0, width, chunk):
        there = slice(at, at + chunk)
        total = jnp.dot(grad_gate, gate_turned_ref[:, there], preferred_element_type=F32)
        turned_ref, start = (low_turned_ref, at) if at < width // 2 else (high_turned_ref, at - width // 2)
        total += jnp.dot(grad_up, turned_ref[:, start : start + chunk], preferred_element_type=F32)
        keep_ref[:, there] = total[:half]
        send_ref[:, there] = total[half:]


def expert(table, hidden_grad, gate, up, low_turned, high_turned, blocks):
    cap, hidden = hidden_grad.shape
    width = gate.shape[0]
    return pl.pallas_call(
        functools.partial(expert_kernel, n_blocks=len(blocks), chunk=512),
        out_shape=(
            jax.ShapeDtypeStruct((cap, width), BF16),
            jax.ShapeDtypeStruct((cap, hidden), BF16),
            jax.ShapeDtypeStruct((cap // 2, width), F32),
            jax.ShapeDtypeStruct((cap // 2, width), F32),
        ),
        in_specs=[VMEM] * (6 + len(blocks)),
        out_specs=(VMEM,) * 4,
        scratch_shapes=[pltpu.VMEM((hidden, width), BF16)],
        compiler_params=pltpu.CompilerParams(vmem_limit_bytes=16 << 20),
        cost_estimate=pl.CostEstimate(
            flops=8 * cap * width * hidden, bytes_accessed=4 * width * hidden, transcendentals=cap * hidden
        ),
        name="expert",
    )(table, hidden_grad, gate, up, low_turned, high_turned, *blocks)


def weight_kernel(slots_ref, grad_ref, *refs, low, high, chunk):
    out_hbm, out_ref, sems = refs[-3:]
    copies = []
    for number, at in enumerate(range(low, high, chunk)):
        there = slice(at - low, at - low + chunk)
        out_ref[there, :] = lax.dot_general(
            slots_ref[:, at : at + chunk], grad_ref[...], (((0,), (0,)), ((), ())), preferred_element_type=F32
        ).astype(out_ref.dtype)
        copies.append(pltpu.make_async_copy(out_ref.at[there, :], out_hbm.at[at : at + chunk, :], sems.at[number]))
        copies[-1].start()
    for copy in copies:
        copy.wait()


def weight_gradient(slots, grad_gate, low, high, out=None):
    cap, width = slots.shape
    hidden = grad_gate.shape[1]
    chunk = 256
    return pl.pallas_call(
        functools.partial(weight_kernel, low=low, high=high, chunk=chunk),
        out_shape=jax.ShapeDtypeStruct((width, hidden), BF16),
        in_specs=[VMEM, VMEM] + ([] if out is None else [HBM]),
        out_specs=HBM,
        scratch_shapes=[
            pltpu.VMEM((high - low, hidden), BF16),
            pltpu.SemaphoreType.DMA(((high - low) // chunk,)),
        ],
        input_output_aliases={} if out is None else {2: 0},
        compiler_params=pltpu.CompilerParams(vmem_limit_bytes=12 << 20),
        cost_estimate=pl.CostEstimate(
            flops=2 * cap * (high - low) * hidden, bytes_accessed=2 * (high - low) * hidden, transcendentals=0
        ),
        name="weight_gradient",
    )(slots, grad_gate, *([] if out is None else [out]))


def per_device(layer_input, hidden_grad, gate_weight, up_weight, expert_ids):
    tok_dev = layer_input.shape[1]
    k_dev = tok_dev // 2
    width = gate_weight.shape[1]
    hids = lax.axis_size("hid")
    split = hids == CORES * CHIPS
    core_at = lax.axis_index("hid") % CORES
    own, gate, up = layer_input[0], gate_weight[0], up_weight[0]
    ids = jnp.swapaxes(expert_ids, 1, 2)

    if split:
        start = opening(4 * gate.size)
        other = to_other_core(own)
        both = pack(ids, own, other, start, k_dev)
        far = moved(both, lambda section, hid: (section, hid ^ (6 if hid % CORES else 2)))
        near = moved(both, lambda section, hid: (section, hid ^ 4))
        after = both
        columns = 4 * tok_dev
    else:
        after = own
        columns = hids * tok_dev
    table, hidden_ordered, pick, low_turned = prepare(
        ids, hidden_grad[0], gate, up, after, columns, tok_dev, k_dev, split
    )
    if split:
        far, low_turned = lax.optimization_barrier((far, low_turned))
        high_turned = turned(up, far, width // 2)
        blocks = [both, near, far, to_other_core(far)]
    else:
        high_turned = turned(up, own, width // 2)
        blocks = [lax.all_gather(own, "hid", axis=0, tiled=True)]
    slots, grad_gate, keep, send = expert(table, hidden_ordered, gate, up, low_turned, high_turned, blocks)
    if split:
        rows = keep.shape[0] // 2
        partner = to_other_core(send)
        weight_grad = weight_gradient(slots, grad_gate, 0, 2 * width // 16)
        partner, weight_grad = lax.optimization_barrier((partner, weight_grad))
        keep = keep + partner
        keep, slots, grad_gate = lax.optimization_barrier((keep, slots, grad_gate))
        across = moved(keep[rows:].astype(BF16), lambda section, hid: (section, hid ^ 2))
        weight_grad = weight_gradient(slots, grad_gate, 2 * width // 16, 13 * width // 16, weight_grad)
        across, weight_grad = lax.optimization_barrier((across, weight_grad))
        part = (keep[:rows] + across.astype(F32)).astype(BF16)
        part, slots = lax.optimization_barrier((part, slots))
        part = moved(part, lambda section, hid: (section - 1, hid ^ (4 * (hid % CORES))))
        weight_grad = weight_gradient(slots, grad_gate, 13 * width // 16, 16 * width // 16, weight_grad)
        part, weight_grad = lax.optimization_barrier((part, weight_grad))
        other = to_other_core(part)
        total = part.astype(F32) + other.astype(F32)
        own_total = jnp.where(core_at == 0, total[:k_dev], total[k_dev:])
    else:
        weight_grad = weight_gradient(slots, grad_gate, 0, width)
        whole = jnp.concatenate([keep, send], axis=0)
        own_total = lax.psum_scatter(whole, "hid", scatter_dimension=0, tiled=True)
        own_total = moved(own_total, lambda section, hid: (section - 1, hid))
    grad_in = jnp.zeros((tok_dev, own.shape[1]), F32)
    for rank in range(k_dev):
        grad_in = jnp.where(pick[:, :1] == rank, own_total[rank : rank + 1], grad_in)
    return (grad_in.astype(BF16)[None], weight_grad[None])


def solution(mesh):
    return jax.shard_map(
        per_device,
        mesh=mesh,
        in_specs=(
            P("section", "hid", None),
            P("section", None, "hid"),
            P("section", None, "hid"),
            P("section", None, "hid"),
            P(),
        ),
        out_specs=(P("section", "hid", None), P("section", None, "hid")),
        check_vma=False,
    )
```

```python
import functools

import jax
import jax.numpy as jnp
from jax import lax
from jax.experimental import pallas as pl
from jax.experimental.pallas import tpu as pltpu
from jax.sharding import PartitionSpec as P

F32 = jnp.float32
BF16 = jnp.bfloat16
CORES = 2
CHIPS = 4
VMEM = pl.BlockSpec(memory_space=pltpu.VMEM)
HBM = pl.BlockSpec(memory_space=pltpu.HBM)
ANY = pl.BlockSpec(memory_space=pl.ANY)


def moved(value, target):
    sections, hids = lax.axis_size("section"), lax.axis_size("hid")
    pairs = []
    for section in range(sections):
        for hid in range(hids):
            to_section, to_hid = target(section, hid)
            pairs.append((section * hids + hid, (to_section % sections) * hids + to_hid))
    return lax.ppermute(value, ("section", "hid"), pairs)


def to_other_core(value):
    return moved(value, lambda section, hid: (section, hid ^ 1))


def lanes(shape, dimension=1):
    return lax.broadcasted_iota(jnp.int32, shape, dimension)


def slot_row(ids_ref, section, tok_dev, k_dev):
    ids = ids_ref[pl.ds(section, 1)][0]
    tokens = ids.shape[1]
    chosen = jnp.where((ids[0:1] == 0) | (ids[1:2] == 0), 1.0, 0.0)
    chosen = jnp.broadcast_to(chosen, (8, tokens))
    before, after = lanes((tokens, tokens), 0), lanes((tokens, tokens), 1)
    earlier = jnp.where((before // tok_dev == after // tok_dev) & (before < after), 1.0, 0.0)
    rank = jnp.dot(chosen.astype(BF16), earlier.astype(BF16), preferred_element_type=F32)
    owner = (lanes((8, tokens)) // tok_dev).astype(F32)
    return jnp.where(chosen > 0, owner * k_dev + rank, -1.0)


def slot_at(slot_of, token):
    tokens = slot_of.shape[1]
    place = jnp.where(lanes((tokens, token.shape[1]), 0) == token, 1.0, 0.0).astype(BF16)
    return jnp.dot(slot_of.astype(BF16), place, preferred_element_type=F32)[0:1]


def pack_table_kernel(ids_ref, after_ref, table_ref, *, tok_dev, k_dev):
    del after_ref
    hid_at = lax.axis_index("hid")
    slot_of = slot_row(ids_ref, lax.axis_index("section"), tok_dev, k_dev)
    column = lanes((1, 2 * tok_dev))
    slots = slot_at(slot_of, (hid_at ^ (column // tok_dev)) * tok_dev + column % tok_dev)
    row = lanes((2 * k_dev, 1), 0)
    wanted = (hid_at ^ (row // k_dev)) * k_dev + row % k_dev
    table_ref[...] = jnp.where(wanted.astype(F32) == slots, 1.0, 0.0).astype(BF16)


def pack_table(ids, after, tok_dev, k_dev):
    return pl.pallas_call(
        functools.partial(pack_table_kernel, tok_dev=tok_dev, k_dev=k_dev),
        out_shape=jax.ShapeDtypeStruct((2 * k_dev, 2 * tok_dev), BF16),
        in_specs=[VMEM, ANY],
        out_specs=VMEM,
        compiler_params=pltpu.CompilerParams(vmem_limit_bytes=4 << 20),
        name="pack_table",
    )(ids, after)


def pack_kernel(table_ref, own_ref, other_ref, out_ref):
    rows = jnp.concatenate([own_ref[...].astype(F32), other_ref[...].astype(F32)], axis=0)
    out_ref[...] = jnp.dot(table_ref[...], rows.astype(BF16), preferred_element_type=F32).astype(BF16)


def pack(table, own, other):
    return pl.pallas_call(
        pack_kernel,
        out_shape=jax.ShapeDtypeStruct((table.shape[0], own.shape[1]), BF16),
        in_specs=[VMEM] * 3,
        out_specs=VMEM,
        compiler_params=pltpu.CompilerParams(vmem_limit_bytes=4 << 20),
        name="pack",
    )(table, own, other)


def open_kernel(out_ref):
    out_ref[...] = jnp.zeros_like(out_ref)


def opening(weight_bytes):
    return pl.pallas_call(
        open_kernel,
        out_shape=jax.ShapeDtypeStruct((8, 128), F32),
        out_specs=VMEM,
        compiler_params=pltpu.CompilerParams(vmem_limit_bytes=1 << 20),
        cost_estimate=pl.CostEstimate(flops=1000 * weight_bytes, bytes_accessed=2 * weight_bytes, transcendentals=0),
        name="opening",
    )()


def prepare_kernel(
    ids_ref, hidden_ref, gate_ref, up_ref, after_ref, table_ref, hidden_out_ref, pick_ref, up_turned_ref,
    *, tok_dev, k_dev, split, chunk,
):
    del gate_ref, after_ref
    for at in range(0, up_turned_ref.shape[1], chunk):
        up_turned_ref[:, at : at + chunk] = up_ref[at : at + chunk, :].T
    section_at, hid_at = lax.axis_index("section"), lax.axis_index("hid")
    core_at, chip_at = hid_at % CORES, hid_at // CORES
    cap, columns = table_ref.shape

    row = lanes((cap, 1), 0)
    device, rank = row // k_dev, row % k_dev
    if split:
        quarter = device // CORES
        step = 2 * jnp.where(quarter < 2, core_at, 1 - core_at) + quarter % 2
        device = (chip_at ^ step) * CORES + device % CORES
    wanted = device * k_dev + rank

    column = lanes((1, columns))
    if split:
        group, place = column // tok_dev, column % tok_dev
        turn = jnp.where(group < 2, 4 * group, jnp.where(group == 2, 2 + 4 * core_at, 7 - 4 * core_at))
        slots = (hid_at ^ turn ^ (place // k_dev)) * k_dev + place % k_dev
    else:
        slots = slot_at(slot_row(ids_ref, section_at, tok_dev, k_dev), column).astype(jnp.int32)
    table_ref[...] = jnp.where(wanted == slots, 1.0, 0.0).astype(BF16)

    order = jnp.where(wanted == lanes((cap, cap)), 1.0, 0.0).astype(BF16)
    hidden_out_ref[...] = jnp.dot(order, hidden_ref[...], preferred_element_type=F32).astype(BF16)

    sections = ids_ref.shape[0]
    slot_of = slot_row(ids_ref, (section_at + 1) % sections, tok_dev, k_dev)[0:1]
    token = lanes((tok_dev, slot_of.shape[1]), 0) + hid_at * tok_dev
    mine = jnp.where(lanes(token.shape) == token, slot_of, 0.0)
    mine = jnp.sum(mine, axis=1, keepdims=True) - (hid_at * k_dev).astype(F32)
    pick_ref[...] = jnp.broadcast_to(mine, pick_ref.shape)


def prepare(ids, hidden_grad, gate, up, after, columns, tok_dev, k_dev, split):
    cap, hidden = hidden_grad.shape
    return pl.pallas_call(
        functools.partial(prepare_kernel, tok_dev=tok_dev, k_dev=k_dev, split=split, chunk=512),
        out_shape=(
            jax.ShapeDtypeStruct((cap, columns), BF16),
            jax.ShapeDtypeStruct((cap, hidden), BF16),
            jax.ShapeDtypeStruct((tok_dev, 128), F32),
            jax.ShapeDtypeStruct((hidden, gate.shape[0] // 2), BF16),
        ),
        in_specs=[VMEM] * 4 + [ANY],
        out_specs=(VMEM,) * 4,
        compiler_params=pltpu.CompilerParams(vmem_limit_bytes=4 << 20),
        cost_estimate=pl.CostEstimate(flops=0, bytes_accessed=4 * gate.size, transcendentals=0),
        name="prepare",
    )(ids, hidden_grad, gate, up, after)


def turn_kernel(weight_ref, after_ref, out_ref, *, low, chunk):
    del after_ref
    for at in range(0, out_ref.shape[1], chunk):
        out_ref[:, at : at + chunk] = weight_ref[low + at : low + at + chunk, :].T


def turned(weight, after, low):
    width, hidden = weight.shape
    return pl.pallas_call(
        functools.partial(turn_kernel, low=low, chunk=512),
        out_shape=jax.ShapeDtypeStruct((hidden, width - low), BF16),
        in_specs=[VMEM, ANY],
        out_specs=VMEM,
        compiler_params=pltpu.CompilerParams(vmem_limit_bytes=4 << 20),
        cost_estimate=pl.CostEstimate(flops=0, bytes_accessed=4 * hidden * (width - low), transcendentals=0),
        name="turn",
    )(weight, after)


def expert_kernel(
    table_ref, hidden_ref, gate_ref, up_ref, low_turned_ref, high_turned_ref, *refs, n_blocks, chunk
):
    block_refs = refs[:n_blocks]
    slots_ref, grad_gate_ref, keep_ref, send_ref, gate_turned_ref = refs[n_blocks:]
    rows = jnp.concatenate([ref[...].astype(F32) for ref in block_refs], axis=0).astype(BF16)
    slots = jnp.dot(table_ref[...], rows, preferred_element_type=F32).astype(BF16)
    slots_ref[...] = slots
    cap, width = slots.shape
    half = cap // 2
    gate_act = jnp.zeros((cap, gate_ref.shape[1]), F32)
    up_act = jnp.zeros((cap, gate_ref.shape[1]), F32)
    for at in range(0, width, chunk):
        part = slots[:, at : at + chunk]
        gate_act += jnp.dot(part, gate_ref[at : at + chunk, :], preferred_element_type=F32)
        up_act += jnp.dot(part, up_ref[at : at + chunk, :], preferred_element_type=F32)
        gate_turned_ref[:, at : at + chunk] = gate_ref[at : at + chunk, :].T
    sigmoid_gate = jax.nn.sigmoid(gate_act)
    hidden_float = hidden_ref[...].astype(F32)
    grad_gate = (
        hidden_float * up_act * sigmoid_gate * (1.0 + gate_act * (1.0 - sigmoid_gate))
    ).astype(BF16)
    grad_up = (hidden_float * gate_act * sigmoid_gate).astype(BF16)
    grad_gate_ref[...] = grad_gate
    for at in range(0, width, chunk):
        there = slice(at, at + chunk)
        total = jnp.dot(grad_gate, gate_turned_ref[:, there], preferred_element_type=F32)
        turned_ref, start = (low_turned_ref, at) if at < width // 2 else (high_turned_ref, at - width // 2)
        total += jnp.dot(grad_up, turned_ref[:, start : start + chunk], preferred_element_type=F32)
        keep_ref[:, there] = total[:half]
        send_ref[:, there] = total[half:]


def expert(table, hidden_grad, gate, up, low_turned, high_turned, blocks):
    cap, hidden = hidden_grad.shape
    width = gate.shape[0]
    return pl.pallas_call(
        functools.partial(expert_kernel, n_blocks=len(blocks), chunk=512),
        out_shape=(
            jax.ShapeDtypeStruct((cap, width), BF16),
            jax.ShapeDtypeStruct((cap, hidden), BF16),
            jax.ShapeDtypeStruct((cap // 2, width), F32),
            jax.ShapeDtypeStruct((cap // 2, width), F32),
        ),
        in_specs=[VMEM] * (6 + len(blocks)),
        out_specs=(VMEM,) * 4,
        scratch_shapes=[pltpu.VMEM((hidden, width), BF16)],
        compiler_params=pltpu.CompilerParams(vmem_limit_bytes=16 << 20),
        cost_estimate=pl.CostEstimate(
            flops=8 * cap * width * hidden, bytes_accessed=4 * width * hidden, transcendentals=cap * hidden
        ),
        name="expert",
    )(table, hidden_grad, gate, up, low_turned, high_turned, *blocks)


def weight_kernel(slots_ref, grad_ref, *refs, low, high, chunk):
    out_hbm, out_ref, sems = refs[-3:]
    copies = []
    for number, at in enumerate(range(low, high, chunk)):
        there = slice(at - low, at - low + chunk)
        out_ref[there, :] = lax.dot_general(
            slots_ref[:, at : at + chunk], grad_ref[...], (((0,), (0,)), ((), ())), preferred_element_type=F32
        ).astype(out_ref.dtype)
        copies.append(pltpu.make_async_copy(out_ref.at[there, :], out_hbm.at[at : at + chunk, :], sems.at[number]))
        copies[-1].start()
    for copy in copies:
        copy.wait()


def weight_gradient(slots, grad_gate, low, high, out=None):
    cap, width = slots.shape
    hidden = grad_gate.shape[1]
    chunk = 256
    return pl.pallas_call(
        functools.partial(weight_kernel, low=low, high=high, chunk=chunk),
        out_shape=jax.ShapeDtypeStruct((width, hidden), BF16),
        in_specs=[VMEM, VMEM] + ([] if out is None else [HBM]),
        out_specs=HBM,
        scratch_shapes=[
            pltpu.VMEM((high - low, hidden), BF16),
            pltpu.SemaphoreType.DMA(((high - low) // chunk,)),
        ],
        input_output_aliases={} if out is None else {2: 0},
        compiler_params=pltpu.CompilerParams(vmem_limit_bytes=12 << 20),
        cost_estimate=pl.CostEstimate(
            flops=2 * cap * (high - low) * hidden, bytes_accessed=2 * (high - low) * hidden, transcendentals=0
        ),
        name="weight_gradient",
    )(slots, grad_gate, *([] if out is None else [out]))


def per_device(layer_input, hidden_grad, gate_weight, up_weight, expert_ids):
    tok_dev = layer_input.shape[1]
    k_dev = tok_dev // 2
    width = gate_weight.shape[1]
    hids = lax.axis_size("hid")
    split = hids == CORES * CHIPS
    core_at = lax.axis_index("hid") % CORES
    own, gate, up = layer_input[0], gate_weight[0], up_weight[0]
    ids = jnp.swapaxes(expert_ids, 1, 2)

    if split:
        start = opening(4 * gate.size)
        other = to_other_core(own)
        both = pack(pack_table(ids, start, tok_dev, k_dev), own, other)
        far = moved(both, lambda section, hid: (section, hid ^ (6 if hid % CORES else 2)))
        near = moved(both, lambda section, hid: (section, hid ^ 4))
        after = both
        columns = 4 * tok_dev
    else:
        after = own
        columns = hids * tok_dev
    table, hidden_ordered, pick, low_turned = prepare(
        ids, hidden_grad[0], gate, up, after, columns, tok_dev, k_dev, split
    )
    if split:
        far, low_turned = lax.optimization_barrier((far, low_turned))
        high_turned = turned(up, far, width // 2)
        blocks = [both, near, far, to_other_core(far)]
    else:
        high_turned = turned(up, own, width // 2)
        blocks = [lax.all_gather(own, "hid", axis=0, tiled=True)]
    slots, grad_gate, keep, send = expert(table, hidden_ordered, gate, up, low_turned, high_turned, blocks)
    if split:
        rows = keep.shape[0] // 2
        partner = to_other_core(send)
        weight_grad = weight_gradient(slots, grad_gate, 0, 2 * width // 16)
        partner, weight_grad = lax.optimization_barrier((partner, weight_grad))
        keep = keep + partner
        keep, slots, grad_gate = lax.optimization_barrier((keep, slots, grad_gate))
        across = moved(keep[rows:].astype(BF16), lambda section, hid: (section, hid ^ 2))
        weight_grad = weight_gradient(slots, grad_gate, 2 * width // 16, 13 * width // 16, weight_grad)
        across, weight_grad = lax.optimization_barrier((across, weight_grad))
        part = (keep[:rows] + across.astype(F32)).astype(BF16)
        part, slots = lax.optimization_barrier((part, slots))
        part = moved(part, lambda section, hid: (section - 1, hid ^ (4 * (hid % CORES))))
        weight_grad = weight_gradient(slots, grad_gate, 13 * width // 16, 16 * width // 16, weight_grad)
        part, weight_grad = lax.optimization_barrier((part, weight_grad))
        sent = jnp.where(core_at == 0, part[k_dev:], part[:k_dev])
        mine = jnp.where(core_at == 0, part[:k_dev], part[k_dev:])
        other = to_other_core(sent)
        own_total = mine.astype(F32) + other.astype(F32)
    else:
        weight_grad = weight_gradient(slots, grad_gate, 0, width)
        whole = jnp.concatenate([keep, send], axis=0)
        own_total = lax.psum_scatter(whole, "hid", scatter_dimension=0, tiled=True)
        own_total = moved(own_total, lambda section, hid: (section - 1, hid))
    grad_in = jnp.zeros((tok_dev, own.shape[1]), F32)
    for rank in range(k_dev):
        grad_in = jnp.where(pick[:, :1] == rank, own_total[rank : rank + 1], grad_in)
    return (grad_in.astype(BF16)[None], weight_grad[None])


def solution(mesh):
    return jax.shard_map(
        per_device,
        mesh=mesh,
        in_specs=(
            P("section", "hid", None),
            P("section", None, "hid"),
            P("section", None, "hid"),
            P("section", None, "hid"),
            P(),
        ),
        out_specs=(P("section", "hid", None), P("section", None, "hid")),
        check_vma=False,
    )
```

```python
import functools

import jax
import jax.numpy as jnp
from jax import lax
from jax.experimental import pallas as pl
from jax.experimental.pallas import tpu as pltpu
from jax.sharding import PartitionSpec as P

F32 = jnp.float32
BF16 = jnp.bfloat16
CORES = 2
CHIPS = 4
VMEM = pl.BlockSpec(memory_space=pltpu.VMEM)
HBM = pl.BlockSpec(memory_space=pltpu.HBM)
ANY = pl.BlockSpec(memory_space=pl.ANY)


def moved(value, target):
    sections, hids = lax.axis_size("section"), lax.axis_size("hid")
    pairs = []
    for section in range(sections):
        for hid in range(hids):
            to_section, to_hid = target(section, hid)
            pairs.append((section * hids + hid, (to_section % sections) * hids + to_hid))
    return lax.ppermute(value, ("section", "hid"), pairs)


def to_other_core(value):
    return moved(value, lambda section, hid: (section, hid ^ 1))


def lanes(shape, dimension=1):
    return lax.broadcasted_iota(jnp.int32, shape, dimension)


def slot_row(ids_ref, section, tok_dev, k_dev):
    ids = ids_ref[pl.ds(section, 1)][0]
    tokens = ids.shape[1]
    chosen = jnp.where((ids[0:1] == 0) | (ids[1:2] == 0), 1.0, 0.0)
    chosen = jnp.broadcast_to(chosen, (8, tokens))
    before, after = lanes((tokens, tokens), 0), lanes((tokens, tokens), 1)
    earlier = jnp.where((before // tok_dev == after // tok_dev) & (before < after), 1.0, 0.0)
    rank = jnp.dot(chosen.astype(BF16), earlier.astype(BF16), preferred_element_type=F32)
    owner = (lanes((8, tokens)) // tok_dev).astype(F32)
    return jnp.where(chosen > 0, owner * k_dev + rank, -1.0)


def slot_at(slot_of, token):
    tokens = slot_of.shape[1]
    place = jnp.where(lanes((tokens, token.shape[1]), 0) == token, 1.0, 0.0).astype(BF16)
    return jnp.dot(slot_of.astype(BF16), place, preferred_element_type=F32)[0:1]


def pack_table_kernel(ids_ref, after_ref, table_ref, *, tok_dev, k_dev):
    del after_ref
    hid_at = lax.axis_index("hid")
    slot_of = slot_row(ids_ref, lax.axis_index("section"), tok_dev, k_dev)
    column = lanes((1, 2 * tok_dev))
    slots = slot_at(slot_of, (hid_at ^ (column // tok_dev)) * tok_dev + column % tok_dev)
    row = lanes((2 * k_dev, 1), 0)
    wanted = (hid_at // CORES * CORES + row // k_dev) * k_dev + row % k_dev
    table_ref[...] = jnp.where(wanted.astype(F32) == slots, 1.0, 0.0).astype(BF16)


def pack_table(ids, after, tok_dev, k_dev):
    return pl.pallas_call(
        functools.partial(pack_table_kernel, tok_dev=tok_dev, k_dev=k_dev),
        out_shape=jax.ShapeDtypeStruct((2 * k_dev, 2 * tok_dev), BF16),
        in_specs=[VMEM, ANY],
        out_specs=VMEM,
        compiler_params=pltpu.CompilerParams(vmem_limit_bytes=4 << 20),
        name="pack_table",
    )(ids, after)


def pack_kernel(table_ref, own_ref, other_ref, out_ref):
    rows = jnp.concatenate([own_ref[...].astype(F32), other_ref[...].astype(F32)], axis=0)
    out_ref[...] = jnp.dot(table_ref[...], rows.astype(BF16), preferred_element_type=F32).astype(BF16)


def pack(table, own, other):
    return pl.pallas_call(
        pack_kernel,
        out_shape=jax.ShapeDtypeStruct((table.shape[0], own.shape[1]), BF16),
        in_specs=[VMEM] * 3,
        out_specs=VMEM,
        compiler_params=pltpu.CompilerParams(vmem_limit_bytes=4 << 20),
        name="pack",
    )(table, own, other)


def open_kernel(out_ref):
    out_ref[...] = jnp.zeros_like(out_ref)


def opening(weight_bytes):
    return pl.pallas_call(
        open_kernel,
        out_shape=jax.ShapeDtypeStruct((8, 128), F32),
        out_specs=VMEM,
        compiler_params=pltpu.CompilerParams(vmem_limit_bytes=1 << 20),
        cost_estimate=pl.CostEstimate(flops=1000 * weight_bytes, bytes_accessed=2 * weight_bytes, transcendentals=0),
        name="opening",
    )()


def prepare_kernel(
    ids_ref, hidden_ref, gate_ref, up_ref, after_ref, table_ref, hidden_out_ref, pick_ref, up_turned_ref,
    *, tok_dev, k_dev, split, chunk,
):
    del gate_ref, after_ref
    for at in range(0, up_turned_ref.shape[1], chunk):
        up_turned_ref[:, at : at + chunk] = up_ref[at : at + chunk, :].T
    section_at, hid_at = lax.axis_index("section"), lax.axis_index("hid")
    core_at, chip_at = hid_at % CORES, hid_at // CORES
    cap, columns = table_ref.shape

    row = lanes((cap, 1), 0)
    device, rank = row // k_dev, row % k_dev
    if split:
        quarter = device // CORES
        step = 2 * jnp.where(quarter < 2, core_at, 1 - core_at) + quarter % 2
        device = (chip_at ^ step) * CORES + device % CORES
    wanted = device * k_dev + rank

    if not split:
        slots = slot_at(slot_row(ids_ref, section_at, tok_dev, k_dev), lanes((1, columns)))
        table_ref[...] = jnp.where(wanted.astype(F32) == slots, 1.0, 0.0).astype(BF16)
    else:
        table_ref[...] = jnp.zeros_like(table_ref)

    order = jnp.where(wanted == lanes((cap, cap)), 1.0, 0.0).astype(BF16)
    hidden_out_ref[...] = jnp.dot(order, hidden_ref[...], preferred_element_type=F32).astype(BF16)

    sections = ids_ref.shape[0]
    slot_of = slot_row(ids_ref, (section_at + 1) % sections, tok_dev, k_dev)[0:1]
    token = lanes((tok_dev, slot_of.shape[1]), 0) + hid_at * tok_dev
    mine = jnp.where(lanes(token.shape) == token, slot_of, 0.0)
    mine = jnp.sum(mine, axis=1, keepdims=True) - (hid_at * k_dev).astype(F32)
    pick_ref[...] = jnp.broadcast_to(mine, pick_ref.shape)


def prepare(ids, hidden_grad, gate, up, after, columns, tok_dev, k_dev, split):
    cap, hidden = hidden_grad.shape
    return pl.pallas_call(
        functools.partial(prepare_kernel, tok_dev=tok_dev, k_dev=k_dev, split=split, chunk=512),
        out_shape=(
            jax.ShapeDtypeStruct((cap, columns), BF16),
            jax.ShapeDtypeStruct((cap, hidden), BF16),
            jax.ShapeDtypeStruct((tok_dev, 128), F32),
            jax.ShapeDtypeStruct((hidden, gate.shape[0] // 2), BF16),
        ),
        in_specs=[VMEM] * 4 + [ANY],
        out_specs=(VMEM,) * 4,
        compiler_params=pltpu.CompilerParams(vmem_limit_bytes=4 << 20),
        cost_estimate=pl.CostEstimate(flops=0, bytes_accessed=4 * gate.size, transcendentals=0),
        name="prepare",
    )(ids, hidden_grad, gate, up, after)


def turn_kernel(weight_ref, after_ref, out_ref, *, low, chunk):
    del after_ref
    for at in range(0, out_ref.shape[1], chunk):
        out_ref[:, at : at + chunk] = weight_ref[low + at : low + at + chunk, :].T


def turned(weight, after, low):
    width, hidden = weight.shape
    return pl.pallas_call(
        functools.partial(turn_kernel, low=low, chunk=512),
        out_shape=jax.ShapeDtypeStruct((hidden, width - low), BF16),
        in_specs=[VMEM, ANY],
        out_specs=VMEM,
        compiler_params=pltpu.CompilerParams(vmem_limit_bytes=4 << 20),
        cost_estimate=pl.CostEstimate(flops=0, bytes_accessed=4 * hidden * (width - low), transcendentals=0),
        name="turn",
    )(weight, after)


def expert_kernel(
    table_ref, hidden_ref, gate_ref, up_ref, low_turned_ref, high_turned_ref, *refs, n_blocks, chunk, split
):
    block_refs = refs[:n_blocks]
    slots_ref, grad_gate_ref, keep_ref, send_ref, gate_turned_ref = refs[n_blocks:]
    blocks = [ref[...].astype(F32) for ref in block_refs]
    if split:
        this_chip, second, far, far_other = blocks
        first_core = lax.axis_index("hid") % CORES == 0
        low = jnp.where(first_core, this_chip, second)
        high = jnp.where(first_core, second, this_chip)
        slots = jnp.concatenate([low, far, high, far_other], axis=0).astype(BF16)
    else:
        rows = jnp.concatenate(blocks, axis=0).astype(BF16)
        slots = jnp.dot(table_ref[...], rows, preferred_element_type=F32).astype(BF16)
    slots_ref[...] = slots
    cap, width = slots.shape
    half = cap // 2
    gate_act = jnp.zeros((cap, gate_ref.shape[1]), F32)
    up_act = jnp.zeros((cap, gate_ref.shape[1]), F32)
    for at in range(0, width, chunk):
        part = slots[:, at : at + chunk]
        gate_act += jnp.dot(part, gate_ref[at : at + chunk, :], preferred_element_type=F32)
        up_act += jnp.dot(part, up_ref[at : at + chunk, :], preferred_element_type=F32)
        gate_turned_ref[:, at : at + chunk] = gate_ref[at : at + chunk, :].T
    sigmoid_gate = jax.nn.sigmoid(gate_act)
    hidden_float = hidden_ref[...].astype(F32)
    grad_gate = (
        hidden_float * up_act * sigmoid_gate * (1.0 + gate_act * (1.0 - sigmoid_gate))
    ).astype(BF16)
    grad_up = (hidden_float * gate_act * sigmoid_gate).astype(BF16)
    grad_gate_ref[...] = grad_gate
    for at in range(0, width, chunk):
        there = slice(at, at + chunk)
        total = jnp.dot(grad_gate, gate_turned_ref[:, there], preferred_element_type=F32)
        turned_ref, start = (low_turned_ref, at) if at < width // 2 else (high_turned_ref, at - width // 2)
        total += jnp.dot(grad_up, turned_ref[:, start : start + chunk], preferred_element_type=F32)
        keep_ref[:, there] = total[:half]
        send_ref[:, there] = total[half:]


def expert(table, hidden_grad, gate, up, low_turned, high_turned, blocks, split):
    cap, hidden = hidden_grad.shape
    width = gate.shape[0]
    return pl.pallas_call(
        functools.partial(expert_kernel, n_blocks=len(blocks), chunk=512, split=split),
        out_shape=(
            jax.ShapeDtypeStruct((cap, width), BF16),
            jax.ShapeDtypeStruct((cap, hidden), BF16),
            jax.ShapeDtypeStruct((cap // 2, width), F32),
            jax.ShapeDtypeStruct((cap // 2, width), F32),
        ),
        in_specs=[VMEM] * (6 + len(blocks)),
        out_specs=(VMEM,) * 4,
        scratch_shapes=[pltpu.VMEM((hidden, width), BF16)],
        compiler_params=pltpu.CompilerParams(vmem_limit_bytes=16 << 20),
        cost_estimate=pl.CostEstimate(
            flops=8 * cap * width * hidden, bytes_accessed=4 * width * hidden, transcendentals=cap * hidden
        ),
        name="expert",
    )(table, hidden_grad, gate, up, low_turned, high_turned, *blocks)


def weight_kernel(slots_ref, grad_ref, *refs, low, high, chunk):
    out_hbm, out_ref, sems = refs[-3:]
    copies = []
    for number, at in enumerate(range(low, high, chunk)):
        there = slice(at - low, at - low + chunk)
        out_ref[there, :] = lax.dot_general(
            slots_ref[:, at : at + chunk], grad_ref[...], (((0,), (0,)), ((), ())), preferred_element_type=F32
        ).astype(out_ref.dtype)
        copies.append(pltpu.make_async_copy(out_ref.at[there, :], out_hbm.at[at : at + chunk, :], sems.at[number]))
        copies[-1].start()
    for copy in copies:
        copy.wait()


def weight_gradient(slots, grad_gate, low, high, out=None):
    cap, width = slots.shape
    hidden = grad_gate.shape[1]
    chunk = 256
    return pl.pallas_call(
        functools.partial(weight_kernel, low=low, high=high, chunk=chunk),
        out_shape=jax.ShapeDtypeStruct((width, hidden), BF16),
        in_specs=[VMEM, VMEM] + ([] if out is None else [HBM]),
        out_specs=HBM,
        scratch_shapes=[
            pltpu.VMEM((high - low, hidden), BF16),
            pltpu.SemaphoreType.DMA(((high - low) // chunk,)),
        ],
        input_output_aliases={} if out is None else {2: 0},
        compiler_params=pltpu.CompilerParams(vmem_limit_bytes=12 << 20),
        cost_estimate=pl.CostEstimate(
            flops=2 * cap * (high - low) * hidden, bytes_accessed=2 * (high - low) * hidden, transcendentals=0
        ),
        name="weight_gradient",
    )(slots, grad_gate, *([] if out is None else [out]))


def per_device(layer_input, hidden_grad, gate_weight, up_weight, expert_ids):
    tok_dev = layer_input.shape[1]
    k_dev = tok_dev // 2
    width = gate_weight.shape[1]
    hids = lax.axis_size("hid")
    split = hids == CORES * CHIPS
    core_at = lax.axis_index("hid") % CORES
    own, gate, up = layer_input[0], gate_weight[0], up_weight[0]
    ids = jnp.swapaxes(expert_ids, 1, 2)

    if split:
        start = opening(4 * gate.size)
        other = to_other_core(own)
        both = pack(pack_table(ids, start, tok_dev, k_dev), own, other)
        far = moved(both, lambda section, hid: (section, hid ^ (6 if hid % CORES else 2)))
        near = moved(both, lambda section, hid: (section, hid ^ 4))
        after = both
        columns = 4 * tok_dev
    else:
        after = own
        columns = hids * tok_dev
    table, hidden_ordered, pick, low_turned = prepare(
        ids, hidden_grad[0], gate, up, after, columns, tok_dev, k_dev, split
    )
    if split:
        far, low_turned = lax.optimization_barrier((far, low_turned))
        high_turned = turned(up, far, width // 2)
        blocks = [both, near, far, to_other_core(far)]
    else:
        high_turned = turned(up, own, width // 2)
        blocks = [lax.all_gather(own, "hid", axis=0, tiled=True)]
    slots, grad_gate, keep, send = expert(table, hidden_ordered, gate, up, low_turned, high_turned, blocks, split)
    if split:
        rows = keep.shape[0] // 2
        partner = to_other_core(send)
        weight_grad = weight_gradient(slots, grad_gate, 0, 2 * width // 16)
        partner, weight_grad = lax.optimization_barrier((partner, weight_grad))
        keep = keep + partner
        keep, slots, grad_gate = lax.optimization_barrier((keep, slots, grad_gate))
        across = moved(keep[rows:].astype(BF16), lambda section, hid: (section, hid ^ 2))
        weight_grad = weight_gradient(slots, grad_gate, 2 * width // 16, 13 * width // 16, weight_grad)
        across, weight_grad = lax.optimization_barrier((across, weight_grad))
        part = (keep[:rows] + across.astype(F32)).astype(BF16)
        part, slots = lax.optimization_barrier((part, slots))
        part = moved(part, lambda section, hid: (section - 1, hid ^ (4 * (hid % CORES))))
        weight_grad = weight_gradient(slots, grad_gate, 13 * width // 16, 16 * width // 16, weight_grad)
        part, weight_grad = lax.optimization_barrier((part, weight_grad))
        sent = jnp.where(core_at == 0, part[k_dev:], part[:k_dev])
        mine = jnp.where(core_at == 0, part[:k_dev], part[k_dev:])
        other = to_other_core(sent)
        own_total = mine.astype(F32) + other.astype(F32)
    else:
        weight_grad = weight_gradient(slots, grad_gate, 0, width)
        whole = jnp.concatenate([keep, send], axis=0)
        own_total = lax.psum_scatter(whole, "hid", scatter_dimension=0, tiled=True)
        own_total = moved(own_total, lambda section, hid: (section - 1, hid))
    grad_in = jnp.zeros((tok_dev, own.shape[1]), F32)
    for rank in range(k_dev):
        grad_in = jnp.where(pick[:, :1] == rank, own_total[rank : rank + 1], grad_in)
    return (grad_in.astype(BF16)[None], weight_grad[None])


def solution(mesh):
    return jax.shard_map(
        per_device,
        mesh=mesh,
        in_specs=(
            P("section", "hid", None),
            P("section", None, "hid"),
            P("section", None, "hid"),
            P("section", None, "hid"),
            P(),
        ),
        out_specs=(P("section", "hid", None), P("section", None, "hid")),
        check_vma=False,
    )
```

```python
import functools

import jax
import jax.numpy as jnp
from jax import lax
from jax.experimental import pallas as pl
from jax.experimental.pallas import tpu as pltpu
from jax.sharding import PartitionSpec as P

F32 = jnp.float32
BF16 = jnp.bfloat16
CORES = 2
CHIPS = 4
VMEM = pl.BlockSpec(memory_space=pltpu.VMEM)
HBM = pl.BlockSpec(memory_space=pltpu.HBM)
ANY = pl.BlockSpec(memory_space=pl.ANY)


def moved(value, target):
    sections, hids = lax.axis_size("section"), lax.axis_size("hid")
    pairs = []
    for section in range(sections):
        for hid in range(hids):
            to_section, to_hid = target(section, hid)
            pairs.append((section * hids + hid, (to_section % sections) * hids + to_hid))
    return lax.ppermute(value, ("section", "hid"), pairs)


def to_other_core(value):
    return moved(value, lambda section, hid: (section, hid ^ 1))


def lanes(shape, dimension=1):
    return lax.broadcasted_iota(jnp.int32, shape, dimension)


def slot_row(ids_ref, section, tok_dev, k_dev):
    ids = ids_ref[pl.ds(section, 1)][0]
    tokens = ids.shape[1]
    chosen = jnp.where((ids[0:1] == 0) | (ids[1:2] == 0), 1.0, 0.0)
    chosen = jnp.broadcast_to(chosen, (8, tokens))
    before, after = lanes((tokens, tokens), 0), lanes((tokens, tokens), 1)
    earlier = jnp.where((before // tok_dev == after // tok_dev) & (before < after), 1.0, 0.0)
    rank = jnp.dot(chosen.astype(BF16), earlier.astype(BF16), preferred_element_type=F32)
    owner = (lanes((8, tokens)) // tok_dev).astype(F32)
    return jnp.where(chosen > 0, owner * k_dev + rank, -1.0)


def slot_at(slot_of, token):
    tokens = slot_of.shape[1]
    place = jnp.where(lanes((tokens, token.shape[1]), 0) == token, 1.0, 0.0).astype(BF16)
    return jnp.dot(slot_of.astype(BF16), place, preferred_element_type=F32)[0:1]


def pack_table_kernel(ids_ref, after_ref, table_ref, *, tok_dev, k_dev):
    del after_ref
    hid_at = lax.axis_index("hid")
    slot_of = slot_row(ids_ref, lax.axis_index("section"), tok_dev, k_dev)
    column = lanes((1, 2 * tok_dev))
    slots = slot_at(slot_of, (hid_at ^ (column // tok_dev)) * tok_dev + column % tok_dev)
    row = lanes((2 * k_dev, 1), 0)
    wanted = (hid_at // CORES * CORES + row // k_dev) * k_dev + row % k_dev
    table_ref[...] = jnp.where(wanted.astype(F32) == slots, 1.0, 0.0).astype(BF16)


def pack_table(ids, after, tok_dev, k_dev):
    return pl.pallas_call(
        functools.partial(pack_table_kernel, tok_dev=tok_dev, k_dev=k_dev),
        out_shape=jax.ShapeDtypeStruct((2 * k_dev, 2 * tok_dev), BF16),
        in_specs=[VMEM, ANY],
        out_specs=VMEM,
        compiler_params=pltpu.CompilerParams(vmem_limit_bytes=4 << 20),
        name="pack_table",
    )(ids, after)


def pack_kernel(table_ref, own_ref, other_ref, out_ref):
    rows = jnp.concatenate([own_ref[...].astype(F32), other_ref[...].astype(F32)], axis=0)
    out_ref[...] = jnp.dot(table_ref[...], rows.astype(BF16), preferred_element_type=F32).astype(BF16)


def pack(table, own, other):
    return pl.pallas_call(
        pack_kernel,
        out_shape=jax.ShapeDtypeStruct((table.shape[0], own.shape[1]), BF16),
        in_specs=[VMEM] * 3,
        out_specs=VMEM,
        compiler_params=pltpu.CompilerParams(vmem_limit_bytes=4 << 20),
        name="pack",
    )(table, own, other)


def open_kernel(out_ref):
    out_ref[...] = jnp.zeros_like(out_ref)


def opening(weight_bytes):
    return pl.pallas_call(
        open_kernel,
        out_shape=jax.ShapeDtypeStruct((8, 128), F32),
        out_specs=VMEM,
        compiler_params=pltpu.CompilerParams(vmem_limit_bytes=1 << 20),
        cost_estimate=pl.CostEstimate(flops=1000 * weight_bytes, bytes_accessed=2 * weight_bytes, transcendentals=0),
        name="opening",
    )()


def prepare_kernel(
    ids_ref, hidden_ref, gate_ref, up_ref, after_ref, table_ref, hidden_out_ref, pick_ref, up_turned_ref,
    *, tok_dev, k_dev, split, chunk,
):
    del gate_ref, after_ref
    for at in range(0, up_turned_ref.shape[1], chunk):
        up_turned_ref[:, at : at + chunk] = up_ref[at : at + chunk, :].T
    section_at, hid_at = lax.axis_index("section"), lax.axis_index("hid")
    core_at, chip_at = hid_at % CORES, hid_at // CORES
    cap, columns = table_ref.shape

    row = lanes((cap, 1), 0)
    device, rank = row // k_dev, row % k_dev
    if split:
        quarter = device // CORES
        step = 2 * jnp.where(quarter < 2, core_at, 1 - core_at) + quarter % 2
        device = (chip_at ^ step) * CORES + device % CORES
    wanted = device * k_dev + rank

    if not split:
        slots = slot_at(slot_row(ids_ref, section_at, tok_dev, k_dev), lanes((1, columns)))
        table_ref[...] = jnp.where(wanted.astype(F32) == slots, 1.0, 0.0).astype(BF16)
    else:
        table_ref[...] = jnp.zeros_like(table_ref)

    order = jnp.where(wanted == lanes((cap, cap)), 1.0, 0.0).astype(BF16)
    hidden_out_ref[...] = jnp.dot(order, hidden_ref[...], preferred_element_type=F32).astype(BF16)

    sections = ids_ref.shape[0]
    slot_of = slot_row(ids_ref, (section_at + 1) % sections, tok_dev, k_dev)[0:1]
    token = lanes((tok_dev, slot_of.shape[1]), 0) + hid_at * tok_dev
    mine = jnp.where(lanes(token.shape) == token, slot_of, 0.0)
    mine = jnp.sum(mine, axis=1, keepdims=True) - (hid_at * k_dev).astype(F32)
    pick_ref[...] = jnp.broadcast_to(mine, pick_ref.shape)


def prepare(ids, hidden_grad, gate, up, after, columns, tok_dev, k_dev, split):
    cap, hidden = hidden_grad.shape
    return pl.pallas_call(
        functools.partial(prepare_kernel, tok_dev=tok_dev, k_dev=k_dev, split=split, chunk=512),
        out_shape=(
            jax.ShapeDtypeStruct((cap, columns), BF16),
            jax.ShapeDtypeStruct((cap, hidden), BF16),
            jax.ShapeDtypeStruct((tok_dev, 128), F32),
            jax.ShapeDtypeStruct((hidden, gate.shape[0] // 2), BF16),
        ),
        in_specs=[VMEM] * 4 + [ANY],
        out_specs=(VMEM,) * 4,
        compiler_params=pltpu.CompilerParams(vmem_limit_bytes=4 << 20),
        cost_estimate=pl.CostEstimate(flops=0, bytes_accessed=4 * gate.size, transcendentals=0),
        name="prepare",
    )(ids, hidden_grad, gate, up, after)


def turn_kernel(weight_ref, after_ref, out_ref, *, low, chunk):
    del after_ref
    for at in range(0, out_ref.shape[1], chunk):
        out_ref[:, at : at + chunk] = weight_ref[low + at : low + at + chunk, :].T


def turned(weight, after, low):
    width, hidden = weight.shape
    return pl.pallas_call(
        functools.partial(turn_kernel, low=low, chunk=512),
        out_shape=jax.ShapeDtypeStruct((hidden, width - low), BF16),
        in_specs=[VMEM, ANY],
        out_specs=VMEM,
        compiler_params=pltpu.CompilerParams(vmem_limit_bytes=4 << 20),
        cost_estimate=pl.CostEstimate(flops=0, bytes_accessed=4 * hidden * (width - low), transcendentals=0),
        name="turn",
    )(weight, after)


def expert_kernel(
    table_ref, hidden_ref, gate_ref, up_ref, low_turned_ref, high_turned_ref, *refs, n_blocks, chunk, split
):
    block_refs = refs[:n_blocks]
    slots_ref, grad_gate_ref, keep_ref, send_ref, gate_turned_ref = refs[n_blocks:]
    blocks = [ref[...].astype(F32) for ref in block_refs]
    if split:
        this_chip, second, far, far_other = blocks
        first_core = lax.axis_index("hid") % CORES == 0
        low = jnp.where(first_core, this_chip, second)
        high = jnp.where(first_core, second, this_chip)
        slots = jnp.concatenate([low, far, high, far_other], axis=0).astype(BF16)
    else:
        rows = jnp.concatenate(blocks, axis=0).astype(BF16)
        slots = jnp.dot(table_ref[...], rows, preferred_element_type=F32).astype(BF16)
    slots_ref[...] = slots
    cap, width = slots.shape
    half = cap // 2
    gate_act = jnp.zeros((cap, gate_ref.shape[1]), F32)
    up_act = jnp.zeros((cap, gate_ref.shape[1]), F32)
    for at in range(0, width, chunk):
        part = slots[:, at : at + chunk]
        gate_act += jnp.dot(part, gate_ref[at : at + chunk, :], preferred_element_type=F32)
        up_act += jnp.dot(part, up_ref[at : at + chunk, :], preferred_element_type=F32)
        gate_turned_ref[:, at : at + chunk] = gate_ref[at : at + chunk, :].T
    sigmoid_gate = jax.nn.sigmoid(gate_act)
    hidden_float = hidden_ref[...].astype(F32)
    grad_gate = (
        hidden_float * up_act * sigmoid_gate * (1.0 + gate_act * (1.0 - sigmoid_gate))
    ).astype(BF16)
    grad_up = (hidden_float * gate_act * sigmoid_gate).astype(BF16)
    grad_gate_ref[...] = grad_gate
    for at in range(0, width, chunk):
        there = slice(at, at + chunk)
        total = jnp.dot(grad_gate, gate_turned_ref[:, there], preferred_element_type=F32)
        turned_ref, start = (low_turned_ref, at) if at < width // 2 else (high_turned_ref, at - width // 2)
        total += jnp.dot(grad_up, turned_ref[:, start : start + chunk], preferred_element_type=F32)
        keep_ref[:, there] = total[:half]
        send_ref[:, there] = total[half:]


def expert(table, hidden_grad, gate, up, low_turned, high_turned, blocks, split):
    cap, hidden = hidden_grad.shape
    width = gate.shape[0]
    return pl.pallas_call(
        functools.partial(expert_kernel, n_blocks=len(blocks), chunk=512, split=split),
        out_shape=(
            jax.ShapeDtypeStruct((cap, width), BF16),
            jax.ShapeDtypeStruct((cap, hidden), BF16),
            jax.ShapeDtypeStruct((cap // 2, width), F32),
            jax.ShapeDtypeStruct((cap // 2, width), F32),
        ),
        in_specs=[VMEM] * (6 + len(blocks)),
        out_specs=(VMEM,) * 4,
        scratch_shapes=[pltpu.VMEM((hidden, width), BF16)],
        compiler_params=pltpu.CompilerParams(vmem_limit_bytes=16 << 20),
        cost_estimate=pl.CostEstimate(
            flops=8 * cap * width * hidden, bytes_accessed=4 * width * hidden, transcendentals=cap * hidden
        ),
        name="expert",
    )(table, hidden_grad, gate, up, low_turned, high_turned, *blocks)


def weight_kernel(slots_ref, grad_ref, *refs, low, high, chunk):
    out_hbm, out_ref, sems = refs[-3:]
    copies = []
    for number, at in enumerate(range(low, high, chunk)):
        there = slice(at - low, at - low + chunk)
        out_ref[there, :] = lax.dot_general(
            slots_ref[:, at : at + chunk], grad_ref[...], (((0,), (0,)), ((), ())), preferred_element_type=F32
        ).astype(out_ref.dtype)
        copies.append(pltpu.make_async_copy(out_ref.at[there, :], out_hbm.at[at : at + chunk, :], sems.at[number]))
        copies[-1].start()
    for copy in copies:
        copy.wait()


def weight_gradient(slots, grad_gate, low, high, out=None):
    cap, width = slots.shape
    hidden = grad_gate.shape[1]
    chunk = 256
    return pl.pallas_call(
        functools.partial(weight_kernel, low=low, high=high, chunk=chunk),
        out_shape=jax.ShapeDtypeStruct((width, hidden), BF16),
        in_specs=[VMEM, VMEM] + ([] if out is None else [HBM]),
        out_specs=HBM,
        scratch_shapes=[
            pltpu.VMEM((high - low, hidden), BF16),
            pltpu.SemaphoreType.DMA(((high - low) // chunk,)),
        ],
        input_output_aliases={} if out is None else {2: 0},
        compiler_params=pltpu.CompilerParams(vmem_limit_bytes=12 << 20),
        cost_estimate=pl.CostEstimate(
            flops=2 * cap * (high - low) * hidden, bytes_accessed=2 * (high - low) * hidden, transcendentals=0
        ),
        name="weight_gradient",
    )(slots, grad_gate, *([] if out is None else [out]))


def close_kernel(part_ref, other_ref, pick_ref, out_ref, *, k_dev):
    part = part_ref[...].astype(F32)
    first_core = lax.axis_index("hid") % CORES == 0
    total = jnp.where(first_core, part[:k_dev], part[k_dev:]) + other_ref[...].astype(F32)
    pick = pick_ref[:, :1]
    rows = jnp.zeros(out_ref.shape, F32)
    for rank in range(k_dev):
        rows = jnp.where(pick == rank, total[rank : rank + 1], rows)
    out_ref[...] = rows.astype(out_ref.dtype)


def close(part, other, pick, k_dev):
    return pl.pallas_call(
        functools.partial(close_kernel, k_dev=k_dev),
        out_shape=jax.ShapeDtypeStruct((pick.shape[0], part.shape[1]), BF16),
        in_specs=[VMEM] * 3,
        out_specs=VMEM,
        compiler_params=pltpu.CompilerParams(vmem_limit_bytes=4 << 20),
        name="close",
    )(part, other, pick)


def per_device(layer_input, hidden_grad, gate_weight, up_weight, expert_ids):
    tok_dev = layer_input.shape[1]
    k_dev = tok_dev // 2
    width = gate_weight.shape[1]
    hids = lax.axis_size("hid")
    split = hids == CORES * CHIPS
    core_at = lax.axis_index("hid") % CORES
    own, gate, up = layer_input[0], gate_weight[0], up_weight[0]
    ids = jnp.swapaxes(expert_ids, 1, 2)

    if split:
        start = opening(4 * gate.size)
        other = to_other_core(own)
        both = pack(pack_table(ids, start, tok_dev, k_dev), own, other)
        far = moved(both, lambda section, hid: (section, hid ^ (6 if hid % CORES else 2)))
        near = moved(both, lambda section, hid: (section, hid ^ 4))
        after = both
        columns = 4 * tok_dev
    else:
        after = own
        columns = hids * tok_dev
    table, hidden_ordered, pick, low_turned = prepare(
        ids, hidden_grad[0], gate, up, after, columns, tok_dev, k_dev, split
    )
    if split:
        far, low_turned = lax.optimization_barrier((far, low_turned))
        high_turned = turned(up, far, width // 2)
        blocks = [both, near, far, to_other_core(far)]
    else:
        high_turned = turned(up, own, width // 2)
        blocks = [lax.all_gather(own, "hid", axis=0, tiled=True)]
    slots, grad_gate, keep, send = expert(table, hidden_ordered, gate, up, low_turned, high_turned, blocks, split)
    if split:
        rows = keep.shape[0] // 2
        partner = to_other_core(send)
        weight_grad = weight_gradient(slots, grad_gate, 0, 2 * width // 16)
        partner, weight_grad = lax.optimization_barrier((partner, weight_grad))
        keep = keep + partner
        keep, slots, grad_gate = lax.optimization_barrier((keep, slots, grad_gate))
        across = moved(keep[rows:].astype(BF16), lambda section, hid: (section, hid ^ 2))
        weight_grad = weight_gradient(slots, grad_gate, 2 * width // 16, 13 * width // 16, weight_grad)
        across, weight_grad = lax.optimization_barrier((across, weight_grad))
        part = (keep[:rows] + across.astype(F32)).astype(BF16)
        part, slots = lax.optimization_barrier((part, slots))
        part = moved(part, lambda section, hid: (section - 1, hid ^ (4 * (hid % CORES))))
        weight_grad = weight_gradient(slots, grad_gate, 13 * width // 16, 16 * width // 16, weight_grad)
        part, weight_grad = lax.optimization_barrier((part, weight_grad))
        sent = jnp.where(core_at == 0, part[k_dev:], part[:k_dev])
        other = to_other_core(sent)
        grad_in = close(part, other, pick, k_dev)
    else:
        weight_grad = weight_gradient(slots, grad_gate, 0, width)
        whole = jnp.concatenate([keep, send], axis=0)
        own_total = lax.psum_scatter(whole, "hid", scatter_dimension=0, tiled=True)
        own_total = moved(own_total, lambda section, hid: (section - 1, hid))
        rows = jnp.zeros((tok_dev, own.shape[1]), F32)
        for rank in range(k_dev):
            rows = jnp.where(pick[:, :1] == rank, own_total[rank : rank + 1], rows)
        grad_in = rows.astype(BF16)
    return (grad_in[None], weight_grad[None])


def solution(mesh):
    return jax.shard_map(
        per_device,
        mesh=mesh,
        in_specs=(
            P("section", "hid", None),
            P("section", None, "hid"),
            P("section", None, "hid"),
            P("section", None, "hid"),
            P(),
        ),
        out_specs=(P("section", "hid", None), P("section", None, "hid")),
        check_vma=False,
    )
```
